32 devices in a mesh: ctx: 8 (over y, x, core), tp: 4 (over z).
Axes of the slice: x: 2, y: 2, z: 4, core: 2. Of those that a mesh axis runs over, the one named last changes fastest.
Arguments:
- streams: bfloat16 [3, 2048, 2048], P(None, 'ctx', 'tp'), may hold values from -6 to 6
- short_filter: float32 [3, 7, 2048], P(None, None, 'tp'), may hold values from -2 to 2
- decay_rates: float32 [2048, 16], P('tp'), may hold values from 2.4414063e-05 to 0.05, as said below
- residues: float32 [2048, 16], P('tp'), may hold values from -0.06 to 0.06
- skip_gain: float32 [2048], P('tp'), may hold values from 0.5 to 1.5
- hyena_weight: bfloat16 [2048, 4096], P('tp'), may hold values from -0.1875 to 0.1875
- value_weight: bfloat16 [4096, 2048], P('tp'), may hold values from -0.125 to 0.125
- queries: bfloat16 [2048, 2048], P('ctx', 'tp'), may hold values from -16.5 to 16.5
- key_vectors: bfloat16 [2048, 2048], P('ctx', 'tp'), may hold values from -16.5 to 16.5
Outputs:
- hyena_out: bfloat16 [2048, 4096], P('ctx', 'tp')
- context: bfloat16 [2048, 2048], P('ctx', 'tp')
The draws below stay inside these ranges and needn't reach their ends.
Inputs may be any that keep to these rules, and one draw needn't show every extreme that they name: `decay_rates`: decay rates lie between 1 / 40960 and 0.05.
All inputs are finite; a program needn't handle non-finite values.
Results may differ from the reference program's by a relative error of at most 0.0066.
Values may be sent and summed in bfloat16 or wider, within the bound.
A program may use at most 128 MiB of HBM per device.

```python
import math
import jax
import jax.numpy as jnp
from jax import lax

D = 4096
HC = 2048
MODES = 16
HA = 16
HD = 128
SEQ = 2048


def draw_decay_rates(key, part):
    slow_low = jnp.log(0.05 / SEQ)
    slow_high = jnp.log(2.0 / SEQ)
    slow_rates = jnp.exp(jax.random.uniform(jax.random.fold_in(key, 1), (HC, MODES), jnp.float32, slow_low, slow_high))
    fast_rates = jnp.exp(jax.random.uniform(jax.random.fold_in(key, 2), (HC, MODES), jnp.float32, jnp.log(0.02), jnp.log(0.05)))
    picker = jax.random.uniform(jax.random.fold_in(key, 3), (HC, MODES), jnp.float32)
    share = 0.5
    return jnp.where(picker < share, slow_rates, fast_rates).astype(jnp.float32)


def draw_queries(key, part):
    base = jnp.clip(jax.random.normal(jax.random.fold_in(key, 21), (SEQ, HA, HD), jnp.float32), -6.0, 6.0)
    return base.reshape(SEQ, HA * HD).astype(jnp.bfloat16)


def draw_key_vectors(key, part):
    base = jnp.clip(2.75 * jax.random.normal(jax.random.fold_in(key, 31), (SEQ, HA, HD), jnp.float32), -16.5, 16.5)
    return base.reshape(SEQ, HA * HD).astype(jnp.bfloat16)


def with_spikes(drawn, rng, source, target, parts, factor):
    def block_of(position):
        return (jnp.arange(drawn.shape[position]) // (drawn.shape[position] // parts)).reshape((-1,) + (1,) * (drawn.ndim - 1 - position))

    near = jax.random.permutation(rng, parts)[block_of(target)]
    far = (block_of(target) + parts // 2) % parts
    return jnp.where((block_of(source) == near) | (block_of(source) == far), factor * drawn, drawn)


def steps_of(key, shape, shards, low, high):
    def one(dim, parts):
        draws = jax.random.uniform(jax.random.fold_in(jax.random.fold_in(key, 6), dim), (parts,), jnp.float32, low / len(shards), high / len(shards))
        return jnp.repeat(jnp.exp(draws), shape[dim] // parts).reshape((-1,) + (1,) * (len(shape) - dim - 1))

    gain = one(*shards[0])
    for cut in shards[1:]:
        gain = gain * one(*cut)
    return gain


def centred(own_key, dims, spread, reach, pieces=(), kind=jnp.bfloat16):
    values = spread * jax.random.normal(own_key, dims, jnp.float32)
    if pieces:
        values = values * steps_of(own_key, dims, pieces, -0.22, 0.18)
    return jnp.clip(values, -reach, reach).astype(kind)


def bell_draw_with(key, extent, scale, most, pieces, heavy, kind=jnp.bfloat16):
    values = scale * jax.random.normal(key, extent, jnp.float32)
    if pieces:
        values = values * steps_of(key, extent, pieces, -0.22, 0.18)
    return jnp.clip(with_spikes(values, jax.random.fold_in(key, 3), *heavy), -most, most).astype(kind)


def setup_inputs(seed: int = 0) -> dict:
    splits = jax.random.split(jax.random.key(seed), 10)
    streams = centred(splits[0], (3, SEQ, HC), 1.0, 6.0, ((1, 8), (2, 4)))
    short_filter = centred(splits[1], (3, 7, HC), 7 ** -0.5, 2.0, ((2, 4),), jnp.float32)
    decay_rates = draw_decay_rates(jax.random.fold_in(splits[9], 71), 0)
    residues = centred(splits[3], (HC, MODES), 0.01, 0.06, ((0, 4),), jnp.float32)
    skip_gain = jnp.clip(0.5 + 1.0 * jax.random.uniform(splits[4], (HC,), jnp.float32) ** steps_of(splits[4], (HC,), ((0, 4),), -0.2, 0.2), 0.5, 1.5)
    hyena_weight = bell_draw_with(splits[5], (HC, D), HC ** -0.5, 0.1875, ((0, 4),), (0, 1, 4, 2.0))
    value_weight = bell_draw_with(splits[6], (D, HA * HD), D ** -0.5, 0.125, ((0, 4),), (0, 1, 4, 2.0))
    queries = draw_queries(jax.random.fold_in(splits[9], 71), 0)
    key_vectors = draw_key_vectors(jax.random.fold_in(splits[9], 71), 0)
    return dict(streams=streams, short_filter=short_filter, decay_rates=decay_rates, residues=residues, skip_gain=skip_gain, hyena_weight=hyena_weight, value_weight=value_weight, queries=queries, key_vectors=key_vectors)


def hyena_part(streams, short_filter, decay_rates, residues, skip_gain, hyena_weight):
    widened = streams.astype(jnp.float32)
    padded = jnp.pad(widened, ((0, 0), (6, 0), (0, 0)))
    filtered = jnp.zeros_like(widened)
    for offset in range(7):
        filtered = filtered + short_filter[:, offset, None, :] * padded[:, 6 - offset:6 - offset + SEQ, :]
    gate_part = filtered[0]
    product = filtered[1] * filtered[2]
    lags = jnp.arange(SEQ).astype(jnp.float32)
    kernel = jnp.zeros((SEQ, HC), jnp.float32)
    for mode in range(MODES):
        kernel = kernel + residues[:, mode][None, :] * jnp.exp(-decay_rates[:, mode][None, :] * lags[:, None])
    length = 2 * SEQ
    spectrum = jnp.fft.rfft(product, n=length, axis=0) * jnp.fft.rfft(kernel, n=length, axis=0)
    longconv = jnp.fft.irfft(spectrum, n=length, axis=0)[:SEQ]
    gated = (gate_part * (longconv + skip_gain[None, :] * product)).astype(jnp.bfloat16)
    return jnp.dot(gated, hyena_weight, preferred_element_type=jnp.float32).astype(jnp.bfloat16)

def attention_part(queries, key_vectors, values):
    block_rows = math.gcd(SEQ, 1024)
    block_count = SEQ // block_rows
    scale = 1.0 / math.sqrt(HD)
    query_heads = queries.reshape(SEQ, HA, HD).transpose(1, 0, 2)
    key_heads = key_vectors.reshape(SEQ, HA, HD).transpose(1, 0, 2)
    value_heads = values.reshape(SEQ, HA, HD).transpose(1, 0, 2)
    key_index = jnp.arange(SEQ).astype(jnp.int32)

    def one_block(index):
        head = (index // block_count).astype(jnp.int32)
        first = (index % block_count * block_rows).astype(jnp.int32)
        query_block = lax.dynamic_slice(query_heads, (head, first, jnp.int32(0)), (1, block_rows, HD))[0]
        key_head = lax.dynamic_index_in_dim(key_heads, head, 0, keepdims=False)
        value_head = lax.dynamic_index_in_dim(value_heads, head, 0, keepdims=False)
        scores = jnp.dot(query_block, key_head.T, preferred_element_type=jnp.float32) * scale
        query_index = first + jnp.arange(block_rows).astype(jnp.int32)
        allowed = key_index[None, :] <= query_index[:, None]
        top = lax.optimization_barrier(jnp.max(jnp.where(allowed, scores, -jnp.inf), axis=1))
        weights = jnp.where(allowed, jnp.exp(scores - top[:, None]), 0.0)
        total = lax.optimization_barrier(jnp.sum(weights, axis=1))
        summed = jnp.dot(weights.astype(jnp.bfloat16), value_head, preferred_element_type=jnp.float32)
        return (summed / total[:, None]).astype(jnp.bfloat16)
    blocks = lax.map(one_block, jnp.arange(HA * block_count).astype(jnp.int32))
    return blocks.reshape(HA, SEQ, HD).transpose(1, 0, 2).reshape(SEQ, HA * HD)

def reference(streams, short_filter, decay_rates, residues, skip_gain, hyena_weight, value_weight, queries, key_vectors):
    hyena_out = hyena_part(streams, short_filter, decay_rates, residues, skip_gain, hyena_weight)
    values = jnp.dot(hyena_out, value_weight, preferred_element_type=jnp.float32).astype(jnp.bfloat16)
    context = attention_part(queries, key_vectors, values)
    return (hyena_out, context)
```

```python
import functools
import math

import jax
import jax.numpy as jnp
from jax import lax
from jax.experimental import pallas as pl
from jax.experimental.pallas import tpu as pltpu
from jax.sharding import PartitionSpec as P

HD = 128
LANES = 128
SEGS = 8
HALO = 16
KEYS = 512


def from_behind(value, axis, steps):
    count = lax.axis_size(axis)
    initial, last = (max(0, -steps), min(count, count - steps))
    return lax.ppermute(value, axis, [(source, source + steps) for source in range(initial, last)])


def filter_kernel(prev_ref, streams_ref, taps_ref, rates_ref, gate_ref, u_ref, seg_ref, end_ref, ext):
    rows = streams_ref.shape[1]
    steps = rows // SEGS
    modes = rates_ref.shape[0]
    outs = []
    for s in range(3):
        ext[s, :HALO, :] = prev_ref[s].astype(jnp.float32)
        ext[s, HALO:, :] = streams_ref[s].astype(jnp.float32)
    for s in range(3):
        acc = taps_ref[s, 0:1, :] * ext[s, HALO:, :]
        for j in range(1, 7):
            acc = acc + taps_ref[s, j : j + 1, :] * ext[s, HALO - j : HALO - j + rows, :]
        outs.append(acc)
    gate_ref[...] = outs[0]
    u_ref[...] = outs[1] * outs[2]
    rates = rates_ref[...]
    decay = jnp.exp(-rates)
    factor = [jnp.broadcast_to(decay[n : n + 1], (SEGS, LANES)) for n in range(modes)]
    state = [jnp.zeros((SEGS, LANES), jnp.float32) for _ in range(modes)]
    for step in range(steps):
        here = u_ref[pl.ds(step, SEGS, stride=steps), :]
        for n in range(modes):
            state[n] = state[n] * factor[n] + here
    left = (steps * (SEGS - 1 - lax.broadcasted_iota(jnp.int32, (SEGS, LANES), 0))).astype(jnp.float32)
    for n in range(modes):
        seg_ref[n * SEGS : (n + 1) * SEGS, :] = state[n]
        reach = jnp.exp(-jnp.broadcast_to(rates[n : n + 1], (SEGS, LANES)) * left)
        end_ref[n : n + 1, :] = jnp.sum(reach * state[n], axis=0, keepdims=True)


def mix_kernel(gate_ref, u_ref, seg_ref, inc_ref, rates_ref, res_ref, skip_ref, out_ref, first, mixed):
    rows = u_ref.shape[0]
    steps = rows // SEGS
    modes = rates_ref.shape[0]
    rates = rates_ref[...]
    decay = jnp.exp(-rates)
    hop = jnp.exp(-rates * steps)
    carried = inc_ref[...]
    for seg in range(SEGS):
        first[pl.ds(seg, modes, stride=SEGS), :] = carried
        carried = carried * hop + seg_ref[pl.ds(seg, modes, stride=SEGS), :]
    residue = res_ref[...]
    skip = jnp.broadcast_to(skip_ref[...], (SEGS, LANES))
    factor = [jnp.broadcast_to(decay[n : n + 1], (SEGS, LANES)) for n in range(modes)]
    weight = [jnp.broadcast_to(residue[n : n + 1], (SEGS, LANES)) for n in range(modes)]
    state = [first[n * SEGS : (n + 1) * SEGS, :] for n in range(modes)]
    for step in range(steps):
        where = pl.ds(step, SEGS, stride=steps)
        here = u_ref[where, :]
        terms = [skip * here, None]
        for n in range(modes):
            state[n] = state[n] * factor[n] + here
            term = weight[n] * state[n]
            terms[n % 2] = term if terms[n % 2] is None else terms[n % 2] + term
        mixed[where, :] = gate_ref[where, :] * (terms[0] + terms[1])
    out_ref[...] = mixed[...].astype(jnp.bfloat16)


def hyena_gated(streams, short_filter, rates, residues, skip_gain):
    rows, chans = streams.shape[1:]
    modes = rates.shape[0]
    blocks = chans // LANES
    previous = from_behind(streams[:, rows - HALO :, :], "ctx", 1)
    f32 = jnp.float32
    tok = pl.BlockSpec((rows, LANES), lambda i: (0, i))
    pole = pl.BlockSpec((modes, LANES), lambda i: (0, i))
    seg = pl.BlockSpec((modes * SEGS, LANES), lambda i: (0, i))
    gate, u, seg_state, end_state = pl.pallas_call(
        filter_kernel,
        grid=(blocks,),
        in_specs=[
            pl.BlockSpec((3, HALO, LANES), lambda i: (0, 0, i)),
            pl.BlockSpec((3, rows, LANES), lambda i: (0, 0, i)),
            pl.BlockSpec((3, 7, LANES), lambda i: (0, 0, i)),
            pole,
        ],
        out_specs=[tok, tok, seg, pole],
        out_shape=[
            jax.ShapeDtypeStruct((rows, chans), f32),
            jax.ShapeDtypeStruct((rows, chans), f32),
            jax.ShapeDtypeStruct((modes * SEGS, chans), f32),
            jax.ShapeDtypeStruct((modes, chans), f32),
        ],
        scratch_shapes=[pltpu.VMEM((3, rows + HALO, LANES), f32)],
        cost_estimate=pl.CostEstimate(flops=20_000_000, bytes_accessed=2_500_000, transcendentals=0),
        compiler_params=pltpu.CompilerParams(vmem_limit_bytes=24 * 1024 * 1024),
        name="filter_scan",
    )(previous, streams, short_filter, rates)
    count, mine = lax.axis_size("ctx"), lax.axis_index("ctx")
    ends = lax.all_gather(end_state, "ctx")
    gap = mine - 1 - jnp.arange(count)
    reach = jnp.exp(-rates[None] * (rows * jnp.maximum(gap, 0)).astype(f32)[:, None, None])
    incoming = jnp.sum(jnp.where((gap >= 0)[:, None, None], reach * ends, 0.0), axis=0)
    return pl.pallas_call(
        mix_kernel,
        grid=(blocks,),
        in_specs=[tok, tok, seg, pole, pole, pole, pl.BlockSpec((1, LANES), lambda i: (0, i))],
        out_specs=tok,
        out_shape=jax.ShapeDtypeStruct((rows, chans), jnp.bfloat16),
        scratch_shapes=[pltpu.VMEM((modes * SEGS, LANES), f32), pltpu.VMEM((rows, LANES), f32)],
        cost_estimate=pl.CostEstimate(flops=20_000_000, bytes_accessed=2_500_000, transcendentals=0),
        compiler_params=pltpu.CompilerParams(vmem_limit_bytes=24 * 1024 * 1024),
        name="mix_scan",
    )(gate, u, seg_state, incoming, rates, residues, skip_gain[None])


def attend_kernel(pos_ref, q_ref, k_ref, v_ref, out_ref, acc, top, total):
    rows = q_ref.shape[0]
    scale = 1.0 / math.sqrt(HD)
    start = pos_ref[0] * rows
    queries = q_ref[...]
    acc[...] = jnp.zeros_like(acc)
    top[...] = jnp.full_like(top, -1e30)
    total[...] = jnp.zeros_like(total)
    ahead = lax.broadcasted_iota(jnp.int32, (rows, KEYS), 0) - lax.broadcasted_iota(
        jnp.int32, (rows, KEYS), 1
    )

    def block(index, unused):
        at = pl.multiple_of(index * KEYS, KEYS)
        scores = (
            lax.dot_general(
                queries,
                k_ref[pl.ds(at, KEYS), :],
                (((1,), (1,)), ((), ())),
                preferred_element_type=jnp.float32,
            )
            * scale
        )
        scores = jnp.where(ahead >= at - start, scores, -1e30)
        old = top[:, 0:1]
        new = jnp.maximum(old, jnp.max(scores, axis=1, keepdims=True))
        weights = jnp.exp(scores - new)
        rescale = jnp.exp(old - new)
        total[...] = jnp.broadcast_to(
            total[:, 0:1] * rescale + jnp.sum(weights, axis=1, keepdims=True), total.shape
        )
        top[...] = jnp.broadcast_to(new, top.shape)
        acc[...] = acc[...] * rescale + jnp.dot(
            weights.astype(jnp.bfloat16), v_ref[pl.ds(at, KEYS), :], preferred_element_type=jnp.float32
        )
        return unused

    lax.fori_loop(0, (start + rows + KEYS - 1) // KEYS, block, 0)
    out_ref[...] = (acc[...] / total[...]).astype(jnp.bfloat16)


def causal_attention(queries, keys, values):
    rows, width = queries.shape
    length = keys.shape[0]
    own = pl.BlockSpec((rows, HD), lambda h: (0, h))
    every = pl.BlockSpec((length, HD), lambda h: (0, h))
    return pl.pallas_call(
        attend_kernel,
        grid=(width // HD,),
        in_specs=[pl.BlockSpec(memory_space=pltpu.SMEM), own, every, every],
        out_specs=own,
        out_shape=jax.ShapeDtypeStruct((rows, width), jnp.bfloat16),
        scratch_shapes=[pltpu.VMEM((rows, HD), jnp.float32) for _ in range(3)],
        cost_estimate=pl.CostEstimate(
            flops=4 * rows * length * width, bytes_accessed=4 * length * width, transcendentals=0
        ),
        compiler_params=pltpu.CompilerParams(vmem_limit_bytes=32 * 1024 * 1024),
        name="attend",
    )(lax.axis_index("ctx").astype(jnp.int32)[None], queries, keys, values)


def shards(
    streams,
    short_filter,
    decay_rates,
    residues,
    skip_gain,
    hyena_weight,
    value_weight,
    queries,
    key_vectors,
):
    ctx, tp = lax.axis_size("ctx"), lax.axis_size("tp")
    rows = streams.shape[1]
    chans, width = hyena_weight.shape
    gated = hyena_gated(streams, short_filter, decay_rates.T, residues.T, skip_gain)
    every_key = lax.all_gather(key_vectors, "ctx", axis=0, tiled=True)

    piece = width // tp // ctx
    share = lax.dynamic_index_in_dim(
        hyena_weight.reshape(chans, tp, ctx, piece), lax.axis_index("ctx"), 2, keepdims=False
    ).transpose(1, 0, 2)
    share = lax.all_to_all(share, "tp", split_axis=0, concat_axis=0, tiled=True)
    columns = lax.all_gather(share.reshape(tp * chans, piece), "ctx", axis=1, tiled=True)

    every_channel = lax.all_gather(gated, "tp", axis=1, tiled=True)
    hyena_out = jnp.dot(every_channel, columns, preferred_element_type=jnp.float32).astype(
        jnp.bfloat16
    )
    terms = jnp.dot(hyena_out, value_weight, preferred_element_type=jnp.float32).astype(jnp.bfloat16)
    terms = terms.reshape(rows, tp, -1).transpose(1, 0, 2)
    terms = lax.all_to_all(terms, "tp", split_axis=0, concat_axis=0, tiled=True)
    values = jnp.sum(terms.astype(jnp.float32), axis=0).astype(jnp.bfloat16)
    every_value = lax.all_gather(values, "ctx", axis=0, tiled=True)
    context = causal_attention(queries, every_key, every_value)
    return (hyena_out, context)


def solution(mesh):
    return jax.shard_map(
        shards,
        mesh=mesh,
        in_specs=(
            P(None, "ctx", "tp"),
            P(None, None, "tp"),
            P("tp", None),
            P("tp", None),
            P("tp"),
            P("tp", None),
            P("tp", None),
            P("ctx", "tp"),
            P("ctx", "tp"),
        ),
        out_specs=(P("ctx", "tp"), P("ctx", "tp")),
        check_vma=False,
    )
```

```python
import functools
import math

import jax
import jax.numpy as jnp
from jax import lax
from jax.experimental import pallas as pl
from jax.experimental.pallas import tpu as pltpu
from jax.sharding import PartitionSpec as P

HD = 128
LANES = 128
SEGS = 8
HALO = 16


def from_behind(value, axis, steps):
    count = lax.axis_size(axis)
    initial, last = (max(0, -steps), min(count, count - steps))
    return lax.ppermute(value, axis, [(source, source + steps) for source in range(initial, last)])


def filter_kernel(prev_ref, streams_ref, taps_ref, rates_ref, gate_ref, u_ref, seg_ref, end_ref, ext):
    rows = streams_ref.shape[1]
    steps = rows // SEGS
    modes = rates_ref.shape[0]
    outs = []
    for s in range(3):
        ext[s, :HALO, :] = prev_ref[s].astype(jnp.float32)
        ext[s, HALO:, :] = streams_ref[s].astype(jnp.float32)
    for s in range(3):
        acc = taps_ref[s, 0:1, :] * ext[s, HALO:, :]
        for j in range(1, 7):
            acc = acc + taps_ref[s, j : j + 1, :] * ext[s, HALO - j : HALO - j + rows, :]
        outs.append(acc)
    gate_ref[...] = outs[0]
    u_ref[...] = outs[1] * outs[2]
    rates = rates_ref[...]
    decay = jnp.exp(-rates)
    factor = [jnp.broadcast_to(decay[n : n + 1], (SEGS, LANES)) for n in range(modes)]
    state = [jnp.zeros((SEGS, LANES), jnp.float32) for _ in range(modes)]
    for step in range(steps):
        here = u_ref[pl.ds(step, SEGS, stride=steps), :]
        for n in range(modes):
            state[n] = state[n] * factor[n] + here
    left = (steps * (SEGS - 1 - lax.broadcasted_iota(jnp.int32, (SEGS, LANES), 0))).astype(jnp.float32)
    for n in range(modes):
        seg_ref[n * SEGS : (n + 1) * SEGS, :] = state[n]
        reach = jnp.exp(-jnp.broadcast_to(rates[n : n + 1], (SEGS, LANES)) * left)
        end_ref[n : n + 1, :] = jnp.sum(reach * state[n], axis=0, keepdims=True)


def mix_kernel(gate_ref, u_ref, seg_ref, inc_ref, rates_ref, res_ref, skip_ref, out_ref, first, mixed):
    rows = u_ref.shape[0]
    steps = rows // SEGS
    modes = rates_ref.shape[0]
    rates = rates_ref[...]
    decay = jnp.exp(-rates)
    hop = jnp.exp(-rates * steps)
    carried = inc_ref[...]
    for seg in range(SEGS):
        first[pl.ds(seg, modes, stride=SEGS), :] = carried
        carried = carried * hop + seg_ref[pl.ds(seg, modes, stride=SEGS), :]
    residue = res_ref[...]
    skip = jnp.broadcast_to(skip_ref[...], (SEGS, LANES))
    factor = [jnp.broadcast_to(decay[n : n + 1], (SEGS, LANES)) for n in range(modes)]
    weight = [jnp.broadcast_to(residue[n : n + 1], (SEGS, LANES)) for n in range(modes)]
    state = [first[n * SEGS : (n + 1) * SEGS, :] for n in range(modes)]
    for step in range(steps):
        where = pl.ds(step, SEGS, stride=steps)
        here = u_ref[where, :]
        terms = [skip * here, None]
        for n in range(modes):
            state[n] = state[n] * factor[n] + here
            term = weight[n] * state[n]
            terms[n % 2] = term if terms[n % 2] is None else terms[n % 2] + term
        mixed[where, :] = gate_ref[where, :] * (terms[0] + terms[1])
    out_ref[...] = mixed[...].astype(jnp.bfloat16)


def hyena_gated(streams, short_filter, rates, residues, skip_gain):
    rows, chans = streams.shape[1:]
    modes = rates.shape[0]
    blocks = chans // LANES
    previous = from_behind(streams[:, rows - HALO :, :], "ctx", 1)
    f32 = jnp.float32
    tok = pl.BlockSpec((rows, LANES), lambda i: (0, i))
    pole = pl.BlockSpec((modes, LANES), lambda i: (0, i))
    seg = pl.BlockSpec((modes * SEGS, LANES), lambda i: (0, i))
    gate, u, seg_state, end_state = pl.pallas_call(
        filter_kernel,
        grid=(blocks,),
        in_specs=[
            pl.BlockSpec((3, HALO, LANES), lambda i: (0, 0, i)),
            pl.BlockSpec((3, rows, LANES), lambda i: (0, 0, i)),
            pl.BlockSpec((3, 7, LANES), lambda i: (0, 0, i)),
            pole,
        ],
        out_specs=[tok, tok, seg, pole],
        out_shape=[
            jax.ShapeDtypeStruct((rows, chans), f32),
            jax.ShapeDtypeStruct((rows, chans), f32),
            jax.ShapeDtypeStruct((modes * SEGS, chans), f32),
            jax.ShapeDtypeStruct((modes, chans), f32),
        ],
        scratch_shapes=[pltpu.VMEM((3, rows + HALO, LANES), f32)],
        cost_estimate=pl.CostEstimate(flops=20_000_000, bytes_accessed=2_500_000, transcendentals=0),
        compiler_params=pltpu.CompilerParams(vmem_limit_bytes=24 * 1024 * 1024),
        name="filter_scan",
    )(previous, streams, short_filter, rates)
    count, mine = lax.axis_size("ctx"), lax.axis_index("ctx")
    ends = lax.all_gather(end_state, "ctx")
    gap = mine - 1 - jnp.arange(count)
    reach = jnp.exp(-rates[None] * (rows * jnp.maximum(gap, 0)).astype(f32)[:, None, None])
    incoming = jnp.sum(jnp.where((gap >= 0)[:, None, None], reach * ends, 0.0), axis=0)
    return pl.pallas_call(
        mix_kernel,
        grid=(blocks,),
        in_specs=[tok, tok, seg, pole, pole, pole, pl.BlockSpec((1, LANES), lambda i: (0, i))],
        out_specs=tok,
        out_shape=jax.ShapeDtypeStruct((rows, chans), jnp.bfloat16),
        scratch_shapes=[pltpu.VMEM((modes * SEGS, LANES), f32), pltpu.VMEM((rows, LANES), f32)],
        cost_estimate=pl.CostEstimate(flops=20_000_000, bytes_accessed=2_500_000, transcendentals=0),
        compiler_params=pltpu.CompilerParams(vmem_limit_bytes=24 * 1024 * 1024),
        name="mix_scan",
    )(gate, u, seg_state, incoming, rates, residues, skip_gain[None])


def attend_kernel(
    ctx, tp, terms_ref, q_ref, k_ref, out_ref, parts, vals, acc, top, total, sum_sems, val_sems
):
    rows, width = q_ref.shape
    heads = width // HD
    scale = 1.0 / math.sqrt(HD)
    me, lane = lax.axis_index("ctx"), lax.axis_index("tp")

    barrier = pltpu.get_barrier_semaphore()
    for away in range(1, tp):
        pl.semaphore_signal(
            barrier,
            inc=1,
            device_id={"tp": lax.rem(lane + away, tp)},
            device_id_type=pl.DeviceIdType.MESH,
        )
    for away in range(1, ctx):
        pl.semaphore_signal(
            barrier,
            inc=1,
            device_id={"ctx": lax.rem(me + away, ctx)},
            device_id_type=pl.DeviceIdType.MESH,
        )
    pl.semaphore_wait(barrier, tp - 1 + ctx - 1)

    def columns(owner, head):
        return terms_ref.at[:, pl.ds(pl.multiple_of(owner * width + head * HD, HD), HD)]

    def sum_copy(away, head):
        owner = lax.rem(lane + away, tp)
        return pltpu.make_async_remote_copy(
            src_ref=columns(owner, head),
            dst_ref=parts.at[away - 1, head],
            send_sem=sum_sems.at[0, away - 1, head],
            recv_sem=sum_sems.at[1, away - 1, head],
            device_id={"tp": owner},
            device_id_type=pl.DeviceIdType.MESH,
        )

    def val_copy(ahead, head):
        return pltpu.make_async_remote_copy(
            src_ref=vals.at[0, head],
            dst_ref=vals.at[ahead, head],
            send_sem=val_sems.at[0, ahead, head],
            recv_sem=val_sems.at[1, ahead, head],
            device_id={"ctx": lax.rem(me + ahead, ctx)},
            device_id_type=pl.DeviceIdType.MESH,
        )

    for head in range(heads):
        for away in range(1, tp):
            sum_copy(away, head).start()

    def attend(head):
        here = slice(head * HD, (head + 1) * HD)

        def fold(behind, diagonal):
            at = pl.multiple_of((me - behind) * rows, rows)
            scores = (
                lax.dot_general(
                    q_ref[:, here],
                    k_ref[pl.ds(at, rows), here],
                    (((1,), (1,)), ((), ())),
                    preferred_element_type=jnp.float32,
                )
                * scale
            )
            if diagonal:
                query = lax.broadcasted_iota(jnp.int32, (rows, rows), 0)
                key = lax.broadcasted_iota(jnp.int32, (rows, rows), 1)
                scores = jnp.where(key <= query, scores, -1e30)
                new = jnp.max(scores, axis=1, keepdims=True)
                weights = jnp.exp(scores - new)
                total[...] = jnp.broadcast_to(jnp.sum(weights, axis=1, keepdims=True), total.shape)
                kept = 0.0
            else:
                old = top[:, 0:1]
                new = jnp.maximum(old, jnp.max(scores, axis=1, keepdims=True))
                weights = jnp.exp(scores - new)
                rescale = jnp.exp(old - new)
                total[...] = jnp.broadcast_to(
                    total[:, 0:1] * rescale + jnp.sum(weights, axis=1, keepdims=True), total.shape
                )
                kept = acc[...] * rescale
            top[...] = jnp.broadcast_to(new, top.shape)
            acc[...] = kept + jnp.dot(
                weights.astype(jnp.bfloat16), vals[behind, head], preferred_element_type=jnp.float32
            )

        fold(0, True)

        def earlier(behind, unused):
            val_copy(behind, head).wait_recv()
            fold(behind, False)
            return unused

        lax.fori_loop(1, me + 1, earlier, 0)
        out_ref[:, here] = (acc[...] / total[...]).astype(jnp.bfloat16)

    for head in range(heads):
        value = columns(lane, head)[...].astype(jnp.float32)
        for away in range(1, tp):
            sum_copy(away, head).wait_recv()
            value = value + parts[away - 1, head].astype(jnp.float32)
        vals[0, head] = value.astype(jnp.bfloat16)

        def hand_on(ahead, unused, head=head):
            val_copy(ahead, head).start()
            return unused

        lax.fori_loop(1, ctx - me, hand_on, 0)
        if head >= 1:
            attend(head - 1)
    attend(heads - 1)

    for head in range(heads):
        for away in range(1, tp):
            sum_copy(away, head).wait_send()

        def sent(ahead, unused, head=head):
            val_copy(ahead, head).wait_send()
            return unused

        lax.fori_loop(1, ctx - me, sent, 0)


def sum_and_attend(terms, queries, keys):
    ctx, tp = lax.axis_size("ctx"), lax.axis_size("tp")
    rows, width = queries.shape
    heads = width // HD
    return pl.pallas_call(
        functools.partial(attend_kernel, ctx, tp),
        in_specs=[pl.BlockSpec(memory_space=pltpu.VMEM)] * 3,
        out_specs=pl.BlockSpec(memory_space=pltpu.VMEM),
        out_shape=jax.ShapeDtypeStruct((rows, width), jnp.bfloat16),
        scratch_shapes=[
            pltpu.VMEM((tp - 1, heads, rows, HD), jnp.bfloat16),
            pltpu.VMEM((ctx, heads, rows, HD), jnp.bfloat16),
            pltpu.VMEM((rows, HD), jnp.float32),
            pltpu.VMEM((rows, HD), jnp.float32),
            pltpu.VMEM((rows, HD), jnp.float32),
            pltpu.SemaphoreType.DMA((2, tp - 1, heads)),
            pltpu.SemaphoreType.DMA((2, ctx, heads)),
        ],
        cost_estimate=pl.CostEstimate(
            flops=4 * rows * keys.shape[0] * width,
            bytes_accessed=4 * keys.shape[0] * width,
            transcendentals=0,
        ),
        compiler_params=pltpu.CompilerParams(
            vmem_limit_bytes=40 * 1024 * 1024, collective_id=0, has_side_effects=True
        ),
        name="sum_attend",
    )(terms, queries, keys)


def shards(
    streams,
    short_filter,
    decay_rates,
    residues,
    skip_gain,
    hyena_weight,
    value_weight,
    queries,
    key_vectors,
):
    ctx, tp = lax.axis_size("ctx"), lax.axis_size("tp")
    rows = streams.shape[1]
    chans, width = hyena_weight.shape
    every_key = lax.all_gather(key_vectors, "ctx", axis=0, tiled=True)
    piece = width // tp // ctx
    mine = lax.axis_index("ctx")
    share = jnp.stack(
        [
            lax.dynamic_slice(hyena_weight, (0, (t * ctx + mine) * piece), (chans, piece))
            for t in range(tp)
        ]
    )
    share = lax.all_to_all(share, "tp", split_axis=0, concat_axis=0, tiled=True)
    share, streams = lax.optimization_barrier((share, streams))
    columns = lax.all_gather(share.reshape(tp * chans, piece), "ctx", axis=1, tiled=True)
    gated = hyena_gated(streams, short_filter, decay_rates.T, residues.T, skip_gain)
    every_channel = lax.all_gather(gated, "tp", axis=1, tiled=True)
    every_channel, every_key = lax.optimization_barrier((every_channel, every_key))
    hyena_out = jnp.dot(every_channel, columns, preferred_element_type=jnp.float32).astype(
        jnp.bfloat16
    )
    terms = jnp.dot(hyena_out, value_weight, preferred_element_type=jnp.float32).astype(jnp.bfloat16)
    context = sum_and_attend(terms, queries, every_key)
    return (hyena_out, context)


def solution(mesh):
    return jax.shard_map(
        shards,
        mesh=mesh,
        in_specs=(
            P(None, "ctx", "tp"),
            P(None, None, "tp"),
            P("tp", None),
            P("tp", None),
            P("tp"),
            P("tp", None),
            P("tp", None),
            P("ctx", "tp"),
            P("ctx", "tp"),
        ),
        out_specs=(P("ctx", "tp"), P("ctx", "tp")),
        check_vma=False,
    )
```

```python
import functools
import math

import jax
import jax.numpy as jnp
from jax import lax
from jax.experimental import pallas as pl
from jax.experimental.pallas import tpu as pltpu
from jax.sharding import PartitionSpec as P

HD = 128
LANES = 128
SEGS = 8
HALO = 16


def from_behind(value, axis, steps):
    count = lax.axis_size(axis)
    initial, last = (max(0, -steps), min(count, count - steps))
    return lax.ppermute(value, axis, [(source, source + steps) for source in range(initial, last)])


def filter_kernel(prev_ref, streams_ref, taps_ref, rates_ref, gate_ref, u_ref, seg_ref, end_ref, ext):
    rows = streams_ref.shape[1]
    steps = rows // SEGS
    modes = rates_ref.shape[0]
    outs = []
    for s in range(3):
        ext[s, :HALO, :] = prev_ref[s].astype(jnp.float32)
        ext[s, HALO:, :] = streams_ref[s].astype(jnp.float32)
    for s in range(3):
        acc = taps_ref[s, 0:1, :] * ext[s, HALO:, :]
        for j in range(1, 7):
            acc = acc + taps_ref[s, j : j + 1, :] * ext[s, HALO - j : HALO - j + rows, :]
        outs.append(acc)
    gate_ref[...] = outs[0]
    u_ref[...] = outs[1] * outs[2]
    rates = rates_ref[...]
    decay = jnp.exp(-rates)
    factor = [jnp.broadcast_to(decay[n : n + 1], (SEGS, LANES)) for n in range(modes)]
    state = [jnp.zeros((SEGS, LANES), jnp.float32) for _ in range(modes)]
    for step in range(steps):
        here = u_ref[pl.ds(step, SEGS, stride=steps), :]
        for n in range(modes):
            state[n] = state[n] * factor[n] + here
    left = (steps * (SEGS - 1 - lax.broadcasted_iota(jnp.int32, (SEGS, LANES), 0))).astype(jnp.float32)
    for n in range(modes):
        seg_ref[n * SEGS : (n + 1) * SEGS, :] = state[n]
        reach = jnp.exp(-jnp.broadcast_to(rates[n : n + 1], (SEGS, LANES)) * left)
        end_ref[n : n + 1, :] = jnp.sum(reach * state[n], axis=0, keepdims=True)


def mix_kernel(gate_ref, u_ref, seg_ref, inc_ref, rates_ref, res_ref, skip_ref, out_ref, first, mixed):
    rows = u_ref.shape[0]
    steps = rows // SEGS
    modes = rates_ref.shape[0]
    rates = rates_ref[...]
    decay = jnp.exp(-rates)
    hop = jnp.exp(-rates * steps)
    carried = inc_ref[...]
    for seg in range(SEGS):
        first[pl.ds(seg, modes, stride=SEGS), :] = carried
        carried = carried * hop + seg_ref[pl.ds(seg, modes, stride=SEGS), :]
    residue = res_ref[...]
    skip = jnp.broadcast_to(skip_ref[...], (SEGS, LANES))
    factor = [jnp.broadcast_to(decay[n : n + 1], (SEGS, LANES)) for n in range(modes)]
    weight = [jnp.broadcast_to(residue[n : n + 1], (SEGS, LANES)) for n in range(modes)]
    state = [first[n * SEGS : (n + 1) * SEGS, :] for n in range(modes)]
    for step in range(steps):
        where = pl.ds(step, SEGS, stride=steps)
        here = u_ref[where, :]
        terms = [skip * here, None]
        for n in range(modes):
            state[n] = state[n] * factor[n] + here
            term = weight[n] * state[n]
            terms[n % 2] = term if terms[n % 2] is None else terms[n % 2] + term
        mixed[where, :] = gate_ref[where, :] * (terms[0] + terms[1])
    out_ref[...] = mixed[...].astype(jnp.bfloat16)


def hyena_gated(streams, short_filter, rates, residues, skip_gain):
    rows, chans = streams.shape[1:]
    modes = rates.shape[0]
    blocks = chans // LANES
    previous = from_behind(streams[:, rows - HALO :, :], "ctx", 1)
    f32 = jnp.float32
    tok = pl.BlockSpec((rows, LANES), lambda i: (0, i))
    pole = pl.BlockSpec((modes, LANES), lambda i: (0, i))
    seg = pl.BlockSpec((modes * SEGS, LANES), lambda i: (0, i))
    gate, u, seg_state, end_state = pl.pallas_call(
        filter_kernel,
        grid=(blocks,),
        in_specs=[
            pl.BlockSpec((3, HALO, LANES), lambda i: (0, 0, i)),
            pl.BlockSpec((3, rows, LANES), lambda i: (0, 0, i)),
            pl.BlockSpec((3, 7, LANES), lambda i: (0, 0, i)),
            pole,
        ],
        out_specs=[tok, tok, seg, pole],
        out_shape=[
            jax.ShapeDtypeStruct((rows, chans), f32),
            jax.ShapeDtypeStruct((rows, chans), f32),
            jax.ShapeDtypeStruct((modes * SEGS, chans), f32),
            jax.ShapeDtypeStruct((modes, chans), f32),
        ],
        scratch_shapes=[pltpu.VMEM((3, rows + HALO, LANES), f32)],
        cost_estimate=pl.CostEstimate(flops=20_000_000, bytes_accessed=2_500_000, transcendentals=0),
        compiler_params=pltpu.CompilerParams(vmem_limit_bytes=24 * 1024 * 1024),
        name="filter_scan",
    )(previous, streams, short_filter, rates)
    count, mine = lax.axis_size("ctx"), lax.axis_index("ctx")
    ends = lax.all_gather(end_state, "ctx")
    gap = mine - 1 - jnp.arange(count)
    reach = jnp.exp(-rates[None] * (rows * jnp.maximum(gap, 0)).astype(f32)[:, None, None])
    incoming = jnp.sum(jnp.where((gap >= 0)[:, None, None], reach * ends, 0.0), axis=0)
    return pl.pallas_call(
        mix_kernel,
        grid=(blocks,),
        in_specs=[tok, tok, seg, pole, pole, pole, pl.BlockSpec((1, LANES), lambda i: (0, i))],
        out_specs=tok,
        out_shape=jax.ShapeDtypeStruct((rows, chans), jnp.bfloat16),
        scratch_shapes=[pltpu.VMEM((modes * SEGS, LANES), f32), pltpu.VMEM((rows, LANES), f32)],
        cost_estimate=pl.CostEstimate(flops=20_000_000, bytes_accessed=2_500_000, transcendentals=0),
        compiler_params=pltpu.CompilerParams(vmem_limit_bytes=24 * 1024 * 1024),
        name="mix_scan",
    )(gate, u, seg_state, incoming, rates, residues, skip_gain[None])


def attend_kernel(
    ctx,
    tp,
    gated_ref,
    share_ref,
    weight_ref,
    q_ref,
    own_ref,
    hyena_ref,
    out_ref,
    gat,
    full,
    terms_ref,
    keys,
    parts,
    vals,
    acc,
    top,
    total,
    gat_sems,
    full_sems,
    key_sems,
    sum_sems,
    val_sems,
):
    rows, width = q_ref.shape
    heads = width // HD
    scale = 1.0 / math.sqrt(HD)
    me, lane = lax.axis_index("ctx"), lax.axis_index("tp")

    barrier = pltpu.get_barrier_semaphore()
    for away in range(1, tp):
        pl.semaphore_signal(
            barrier,
            inc=1,
            device_id={"tp": lax.rem(lane + away, tp)},
            device_id_type=pl.DeviceIdType.MESH,
        )
    for away in range(1, ctx):
        pl.semaphore_signal(
            barrier,
            inc=1,
            device_id={"ctx": lax.rem(me + away, ctx)},
            device_id_type=pl.DeviceIdType.MESH,
        )
    pl.semaphore_wait(barrier, tp - 1 + ctx - 1)

    def gat_copy(away):
        return pltpu.make_async_remote_copy(
            src_ref=gated_ref,
            dst_ref=gat.at[lane],
            send_sem=gat_sems.at[0, away],
            recv_sem=gat_sems.at[1, away],
            device_id={"tp": lax.rem(lane + away, tp)},
            device_id_type=pl.DeviceIdType.MESH,
        )

    def full_copy(away):
        return pltpu.make_async_remote_copy(
            src_ref=share_ref,
            dst_ref=full.at[:, me],
            send_sem=full_sems.at[0, away],
            recv_sem=full_sems.at[1, away],
            device_id={"ctx": lax.rem(me + away, ctx)},
            device_id_type=pl.DeviceIdType.MESH,
        )

    def key_copy(ahead):
        return pltpu.make_async_remote_copy(
            src_ref=own_ref,
            dst_ref=keys.at[ahead],
            send_sem=key_sems.at[0, ahead],
            recv_sem=key_sems.at[1, ahead],
            device_id={"ctx": lax.rem(me + ahead, ctx)},
            device_id_type=pl.DeviceIdType.MESH,
        )

    for away in range(1, tp):
        gat_copy(away).start()
    for away in range(1, ctx):
        full_copy(away).start()

    def key_on(ahead, unused):
        key_copy(ahead).start()
        return unused

    lax.fori_loop(1, ctx - me, key_on, 0)
    gat[lane] = gated_ref[...]
    full[:, me] = share_ref[...]
    keys[0] = own_ref[...]
    for away in range(1, tp):
        gat_copy(away).wait_recv()
    for away in range(1, ctx):
        full_copy(away).wait_recv()
    chans, wide = gat.shape[2], full.shape[3]
    tile = min(wide, 256)
    for at in range(0, wide, tile):
        summed = None
        for p in range(tp):
            term = jnp.dot(
                gat[p],
                full[p, :, :, at : at + tile].reshape(chans, tile),
                preferred_element_type=jnp.float32,
            )
            summed = term if summed is None else summed + term
        hyena_ref[:, at : at + tile] = summed.astype(jnp.bfloat16)
    for at in range(0, tp * width, width):
        terms_ref[:, at : at + width] = jnp.dot(
            hyena_ref[...], weight_ref[:, at : at + width], preferred_element_type=jnp.float32
        ).astype(jnp.bfloat16)

    def columns(owner, head):
        return terms_ref.at[:, pl.ds(pl.multiple_of(owner * width + head * HD, HD), HD)]

    def sum_copy(away, head):
        owner = lax.rem(lane + away, tp)
        return pltpu.make_async_remote_copy(
            src_ref=columns(owner, head),
            dst_ref=parts.at[away - 1, head],
            send_sem=sum_sems.at[0, away - 1, head],
            recv_sem=sum_sems.at[1, away - 1, head],
            device_id={"tp": owner},
            device_id_type=pl.DeviceIdType.MESH,
        )

    def val_copy(ahead, head):
        return pltpu.make_async_remote_copy(
            src_ref=vals.at[0, head],
            dst_ref=vals.at[ahead, head],
            send_sem=val_sems.at[0, ahead, head],
            recv_sem=val_sems.at[1, ahead, head],
            device_id={"ctx": lax.rem(me + ahead, ctx)},
            device_id_type=pl.DeviceIdType.MESH,
        )

    for head in range(heads):
        for away in range(1, tp):
            sum_copy(away, head).start()

    def attend(head):
        here = slice(head * HD, (head + 1) * HD)

        def fold(behind, diagonal):
            scores = (
                lax.dot_general(
                    q_ref[:, here],
                    keys[behind, :, here],
                    (((1,), (1,)), ((), ())),
                    preferred_element_type=jnp.float32,
                )
                * scale
            )
            if diagonal:
                query = lax.broadcasted_iota(jnp.int32, (rows, rows), 0)
                key = lax.broadcasted_iota(jnp.int32, (rows, rows), 1)
                scores = jnp.where(key <= query, scores, -1e30)
                new = jnp.max(scores, axis=1, keepdims=True)
                weights = jnp.exp(scores - new)
                total[...] = jnp.broadcast_to(jnp.sum(weights, axis=1, keepdims=True), total.shape)
                kept = 0.0
            else:
                old = top[:, 0:1]
                new = jnp.maximum(old, jnp.max(scores, axis=1, keepdims=True))
                weights = jnp.exp(scores - new)
                rescale = jnp.exp(old - new)
                total[...] = jnp.broadcast_to(
                    total[:, 0:1] * rescale + jnp.sum(weights, axis=1, keepdims=True), total.shape
                )
                kept = acc[...] * rescale
            top[...] = jnp.broadcast_to(new, top.shape)
            acc[...] = kept + jnp.dot(
                weights.astype(jnp.bfloat16), vals[behind, head], preferred_element_type=jnp.float32
            )

        fold(0, True)

        def earlier(behind, unused):
            if head == 0:
                key_copy(behind).wait_recv()
            val_copy(behind, head).wait_recv()
            fold(behind, False)
            return unused

        lax.fori_loop(1, me + 1, earlier, 0)
        out_ref[:, here] = (acc[...] / total[...]).astype(jnp.bfloat16)

    for head in range(heads):
        value = columns(lane, head)[...].astype(jnp.float32)
        for away in range(1, tp):
            sum_copy(away, head).wait_recv()
            value = value + parts[away - 1, head].astype(jnp.float32)
        vals[0, head] = value.astype(jnp.bfloat16)

        def hand_on(ahead, unused, head=head):
            val_copy(ahead, head).start()
            return unused

        lax.fori_loop(1, ctx - me, hand_on, 0)
        if head >= 1:
            attend(head - 1)
    attend(heads - 1)

    for head in range(heads):
        for away in range(1, tp):
            sum_copy(away, head).wait_send()

        def sent(ahead, unused, head=head):
            val_copy(ahead, head).wait_send()
            return unused

        lax.fori_loop(1, ctx - me, sent, 0)
    for away in range(1, tp):
        gat_copy(away).wait_send()
    for away in range(1, ctx):
        full_copy(away).wait_send()

    def key_sent(ahead, unused):
        key_copy(ahead).wait_send()
        return unused

    lax.fori_loop(1, ctx - me, key_sent, 0)


def sum_and_attend(gated, share, value_weight, queries, keys):
    ctx, tp = lax.axis_size("ctx"), lax.axis_size("tp")
    rows, width = queries.shape
    heads = width // HD
    return pl.pallas_call(
        functools.partial(attend_kernel, ctx, tp),
        in_specs=[pl.BlockSpec(memory_space=pltpu.VMEM)] * 5,
        out_specs=[pl.BlockSpec(memory_space=pltpu.VMEM)] * 2,
        out_shape=[
            jax.ShapeDtypeStruct((rows, share.shape[2]), jnp.bfloat16),
            jax.ShapeDtypeStruct((rows, width), jnp.bfloat16),
        ],
        scratch_shapes=[
            pltpu.VMEM((tp,) + gated.shape, jnp.bfloat16),
            pltpu.VMEM((tp, ctx) + share.shape[1:], jnp.bfloat16),
            pltpu.VMEM((rows, tp * width), jnp.bfloat16),
            pltpu.VMEM((ctx, rows, width), jnp.bfloat16),
            pltpu.VMEM((tp - 1, heads, rows, HD), jnp.bfloat16),
            pltpu.VMEM((ctx, heads, rows, HD), jnp.bfloat16),
            pltpu.VMEM((rows, HD), jnp.float32),
            pltpu.VMEM((rows, HD), jnp.float32),
            pltpu.VMEM((rows, HD), jnp.float32),
            pltpu.SemaphoreType.DMA((2, tp)),
            pltpu.SemaphoreType.DMA((2, ctx)),
            pltpu.SemaphoreType.DMA((2, ctx)),
            pltpu.SemaphoreType.DMA((2, tp - 1, heads)),
            pltpu.SemaphoreType.DMA((2, ctx, heads)),
        ],
        cost_estimate=pl.CostEstimate(
            flops=4 * rows * ctx * rows * width,
            bytes_accessed=4 * ctx * rows * width,
            transcendentals=0,
        ),
        compiler_params=pltpu.CompilerParams(
            vmem_limit_bytes=48 * 1024 * 1024, collective_id=0, has_side_effects=True
        ),
        name="sum_attend",
    )(gated, share, value_weight, queries, keys)


def shards(
    streams,
    short_filter,
    decay_rates,
    residues,
    skip_gain,
    hyena_weight,
    value_weight,
    queries,
    key_vectors,
):
    ctx, tp = lax.axis_size("ctx"), lax.axis_size("tp")
    rows = streams.shape[1]
    chans, width = hyena_weight.shape
    part = chans // ctx
    share = lax.dynamic_slice(hyena_weight, (lax.axis_index("ctx") * part, 0), (part, width))
    share = share.reshape(part, tp, width // tp).transpose(1, 0, 2)
    share = lax.all_to_all(share, "tp", split_axis=0, concat_axis=0, tiled=True)
    gated = hyena_gated(streams, short_filter, decay_rates.T, residues.T, skip_gain)
    hyena_out, context = sum_and_attend(gated, share, value_weight, queries, key_vectors)
    return (hyena_out, context)


def solution(mesh):
    return jax.shard_map(
        shards,
        mesh=mesh,
        in_specs=(
            P(None, "ctx", "tp"),
            P(None, None, "tp"),
            P("tp", None),
            P("tp", None),
            P("tp"),
            P("tp", None),
            P("tp", None),
            P("ctx", "tp"),
            P("ctx", "tp"),
        ),
        out_specs=(P("ctx", "tp"), P("ctx", "tp")),
        check_vma=False,
    )
```

```python
import functools
import math

import jax
import jax.numpy as jnp
from jax import lax
from jax.experimental import pallas as pl
from jax.experimental.pallas import tpu as pltpu
from jax.sharding import PartitionSpec as P

HD = 128
LANES = 128
SEGS = 8
HALO = 16


def from_behind(value, axis, steps):
    count = lax.axis_size(axis)
    initial, last = (max(0, -steps), min(count, count - steps))
    return lax.ppermute(value, axis, [(source, source + steps) for source in range(initial, last)])


def filter_kernel(prev_ref, streams_ref, taps_ref, rates_ref, gate_ref, u_ref, seg_ref, end_ref, ext):
    rows = streams_ref.shape[1]
    steps = rows // SEGS
    modes = rates_ref.shape[0]
    outs = []
    for s in range(3):
        ext[s, :HALO, :] = prev_ref[s].astype(jnp.float32)
        ext[s, HALO:, :] = streams_ref[s].astype(jnp.float32)
    for s in range(3):
        acc = taps_ref[s, 0:1, :] * ext[s, HALO:, :]
        for j in range(1, 7):
            acc = acc + taps_ref[s, j : j + 1, :] * ext[s, HALO - j : HALO - j + rows, :]
        outs.append(acc)
    gate_ref[...] = outs[0]
    u_ref[...] = outs[1] * outs[2]
    rates = rates_ref[...]
    decay = jnp.exp(-rates)
    factor = [jnp.broadcast_to(decay[n : n + 1], (SEGS, LANES)) for n in range(modes)]
    state = [jnp.zeros((SEGS, LANES), jnp.float32) for _ in range(modes)]
    for step in range(steps):
        here = u_ref[pl.ds(step, SEGS, stride=steps), :]
        for n in range(modes):
            state[n] = state[n] * factor[n] + here
    left = (steps * (SEGS - 1 - lax.broadcasted_iota(jnp.int32, (SEGS, LANES), 0))).astype(jnp.float32)
    for n in range(modes):
        seg_ref[n * SEGS : (n + 1) * SEGS, :] = state[n]
        reach = jnp.exp(-jnp.broadcast_to(rates[n : n + 1], (SEGS, LANES)) * left)
        end_ref[n : n + 1, :] = jnp.sum(reach * state[n], axis=0, keepdims=True)


def mix_kernel(gate_ref, u_ref, seg_ref, inc_ref, rates_ref, res_ref, skip_ref, out_ref, first, mixed):
    rows = u_ref.shape[0]
    steps = rows // SEGS
    modes = rates_ref.shape[0]
    rates = rates_ref[...]
    decay = jnp.exp(-rates)
    hop = jnp.exp(-rates * steps)
    carried = inc_ref[...]
    for seg in range(SEGS):
        first[pl.ds(seg, modes, stride=SEGS), :] = carried
        carried = carried * hop + seg_ref[pl.ds(seg, modes, stride=SEGS), :]
    residue = res_ref[...]
    skip = jnp.broadcast_to(skip_ref[...], (SEGS, LANES))
    factor = [jnp.broadcast_to(decay[n : n + 1], (SEGS, LANES)) for n in range(modes)]
    weight = [jnp.broadcast_to(residue[n : n + 1], (SEGS, LANES)) for n in range(modes)]
    state = [first[n * SEGS : (n + 1) * SEGS, :] for n in range(modes)]
    for step in range(steps):
        where = pl.ds(step, SEGS, stride=steps)
        here = u_ref[where, :]
        terms = [skip * here, None]
        for n in range(modes):
            state[n] = state[n] * factor[n] + here
            term = weight[n] * state[n]
            terms[n % 2] = term if terms[n % 2] is None else terms[n % 2] + term
        mixed[where, :] = gate_ref[where, :] * (terms[0] + terms[1])
    out_ref[...] = mixed[...].astype(jnp.bfloat16)


def hyena_gated(streams, short_filter, rates, residues, skip_gain):
    rows, chans = streams.shape[1:]
    modes = rates.shape[0]
    blocks = chans // LANES
    previous = from_behind(streams[:, rows - HALO :, :], "ctx", 1)
    f32 = jnp.float32
    tok = pl.BlockSpec((rows, LANES), lambda i: (0, i))
    pole = pl.BlockSpec((modes, LANES), lambda i: (0, i))
    seg = pl.BlockSpec((modes * SEGS, LANES), lambda i: (0, i))
    gate, u, seg_state, end_state = pl.pallas_call(
        filter_kernel,
        grid=(blocks,),
        in_specs=[
            pl.BlockSpec((3, HALO, LANES), lambda i: (0, 0, i)),
            pl.BlockSpec((3, rows, LANES), lambda i: (0, 0, i)),
            pl.BlockSpec((3, 7, LANES), lambda i: (0, 0, i)),
            pole,
        ],
        out_specs=[tok, tok, seg, pole],
        out_shape=[
            jax.ShapeDtypeStruct((rows, chans), f32),
            jax.ShapeDtypeStruct((rows, chans), f32),
            jax.ShapeDtypeStruct((modes * SEGS, chans), f32),
            jax.ShapeDtypeStruct((modes, chans), f32),
        ],
        scratch_shapes=[pltpu.VMEM((3, rows + HALO, LANES), f32)],
        cost_estimate=pl.CostEstimate(flops=20_000_000, bytes_accessed=2_500_000, transcendentals=0),
        compiler_params=pltpu.CompilerParams(vmem_limit_bytes=24 * 1024 * 1024),
        name="filter_scan",
    )(previous, streams, short_filter, rates)
    count, mine = lax.axis_size("ctx"), lax.axis_index("ctx")
    ends = lax.all_gather(end_state, "ctx")
    gap = mine - 1 - jnp.arange(count)
    reach = jnp.exp(-rates[None] * (rows * jnp.maximum(gap, 0)).astype(f32)[:, None, None])
    incoming = jnp.sum(jnp.where((gap >= 0)[:, None, None], reach * ends, 0.0), axis=0)
    return pl.pallas_call(
        mix_kernel,
        grid=(blocks,),
        in_specs=[tok, tok, seg, pole, pole, pole, pl.BlockSpec((1, LANES), lambda i: (0, i))],
        out_specs=tok,
        out_shape=jax.ShapeDtypeStruct((rows, chans), jnp.bfloat16),
        scratch_shapes=[pltpu.VMEM((modes * SEGS, LANES), f32), pltpu.VMEM((rows, LANES), f32)],
        cost_estimate=pl.CostEstimate(flops=20_000_000, bytes_accessed=2_500_000, transcendentals=0),
        compiler_params=pltpu.CompilerParams(vmem_limit_bytes=24 * 1024 * 1024),
        name="mix_scan",
    )(gate, u, seg_state, incoming, rates, residues, skip_gain[None])


def attend_kernel(
    ctx,
    tp,
    gated_ref,
    share_ref,
    weight_ref,
    q_ref,
    own_ref,
    hyena_ref,
    out_ref,
    gat,
    full,
    terms_ref,
    keys,
    parts,
    vals,
    acc,
    top,
    total,
    gat_sems,
    full_sems,
    key_sems,
    sum_sems,
    val_sems,
):
    rows, width = q_ref.shape
    heads = width // HD
    scale = 1.0 / math.sqrt(HD)
    me, lane = lax.axis_index("ctx"), lax.axis_index("tp")

    barrier = pltpu.get_barrier_semaphore()
    for away in range(1, tp):
        pl.semaphore_signal(
            barrier,
            inc=1,
            device_id={"tp": lax.rem(lane + away, tp)},
            device_id_type=pl.DeviceIdType.MESH,
        )
    for away in range(1, ctx):
        pl.semaphore_signal(
            barrier,
            inc=1,
            device_id={"ctx": lax.rem(me + away, ctx)},
            device_id_type=pl.DeviceIdType.MESH,
        )
    pl.semaphore_wait(barrier, tp - 1 + ctx - 1)

    def gat_copy(away):
        return pltpu.make_async_remote_copy(
            src_ref=gated_ref,
            dst_ref=gat.at[lane],
            send_sem=gat_sems.at[0, away],
            recv_sem=gat_sems.at[1, away],
            device_id={"tp": lax.rem(lane + away, tp)},
            device_id_type=pl.DeviceIdType.MESH,
        )

    chips = ctx // 2
    chip, core = lax.div(me, 2), lax.rem(me, 2)
    sibling = 2 * chip + 1 - core

    def full_copy(index):
        if index == 0:
            source, block, target = share_ref, me, sibling
        elif index < chips:
            source, block = share_ref, me
            target = 2 * lax.rem(chip + index, chips) + core
        else:
            away = index - chips + 1
            block = 2 * lax.rem(chip + chips - away, chips) + core
            source, target = full.at[:, block], sibling
        return pltpu.make_async_remote_copy(
            src_ref=source,
            dst_ref=full.at[:, block],
            send_sem=full_sems.at[0, index],
            recv_sem=full_sems.at[1, index],
            device_id={"ctx": target},
            device_id_type=pl.DeviceIdType.MESH,
        )

    def key_copy(ahead):
        return pltpu.make_async_remote_copy(
            src_ref=own_ref,
            dst_ref=keys.at[ahead],
            send_sem=key_sems.at[0, ahead],
            recv_sem=key_sems.at[1, ahead],
            device_id={"ctx": lax.rem(me + ahead, ctx)},
            device_id_type=pl.DeviceIdType.MESH,
        )

    for away in range(1, tp):
        gat_copy(away).start()
    for index in range(1, chips):
        full_copy(index).start()
    full_copy(0).start()

    def key_on(ahead, unused):
        key_copy(ahead).start()
        return unused

    gat[lane] = gated_ref[...]
    full[:, me] = share_ref[...]
    keys[0] = own_ref[...]
    for index in range(1, chips):
        full_copy(index).wait_recv()
        full_copy(index + chips - 1).start()
    lax.fori_loop(1, ctx - me, key_on, 0)
    for away in range(1, tp):
        gat_copy(away).wait_recv()
    full_copy(0).wait_recv()
    for index in range(chips, 2 * chips - 1):
        full_copy(index).wait_recv()
    chans, wide = gat.shape[2], full.shape[3]
    tile = min(wide, 256)
    for at in range(0, wide, tile):
        summed = None
        for p in range(tp):
            term = jnp.dot(
                gat[p],
                full[p, :, :, at : at + tile].reshape(chans, tile),
                preferred_element_type=jnp.float32,
            )
            summed = term if summed is None else summed + term
        hyena_ref[:, at : at + tile] = summed.astype(jnp.bfloat16)
    for at in range(0, tp * width, width):
        terms_ref[:, at : at + width] = jnp.dot(
            hyena_ref[...], weight_ref[:, at : at + width], preferred_element_type=jnp.float32
        ).astype(jnp.bfloat16)

    def columns(owner, head):
        return terms_ref.at[:, pl.ds(pl.multiple_of(owner * width + head * HD, HD), HD)]

    def sum_copy(away, head):
        owner = lax.rem(lane + away, tp)
        return pltpu.make_async_remote_copy(
            src_ref=columns(owner, head),
            dst_ref=parts.at[away - 1, head],
            send_sem=sum_sems.at[0, away - 1, head],
            recv_sem=sum_sems.at[1, away - 1, head],
            device_id={"tp": owner},
            device_id_type=pl.DeviceIdType.MESH,
        )

    def val_copy(ahead, head):
        return pltpu.make_async_remote_copy(
            src_ref=vals.at[0, head],
            dst_ref=vals.at[ahead, head],
            send_sem=val_sems.at[0, ahead, head],
            recv_sem=val_sems.at[1, ahead, head],
            device_id={"ctx": lax.rem(me + ahead, ctx)},
            device_id_type=pl.DeviceIdType.MESH,
        )

    for head in range(heads):
        for away in range(1, tp):
            sum_copy(away, head).start()

    def attend(head):
        here = slice(head * HD, (head + 1) * HD)

        def fold(behind, diagonal):
            scores = (
                lax.dot_general(
                    q_ref[:, here],
                    keys[behind, :, here],
                    (((1,), (1,)), ((), ())),
                    preferred_element_type=jnp.float32,
                )
                * scale
            )
            if diagonal:
                query = lax.broadcasted_iota(jnp.int32, (rows, rows), 0)
                key = lax.broadcasted_iota(jnp.int32, (rows, rows), 1)
                scores = jnp.where(key <= query, scores, -1e30)
                new = jnp.max(scores, axis=1, keepdims=True)
                weights = jnp.exp(scores - new)
                total[...] = jnp.broadcast_to(jnp.sum(weights, axis=1, keepdims=True), total.shape)
                kept = 0.0
            else:
                old = top[:, 0:1]
                new = jnp.maximum(old, jnp.max(scores, axis=1, keepdims=True))
                weights = jnp.exp(scores - new)
                rescale = jnp.exp(old - new)
                total[...] = jnp.broadcast_to(
                    total[:, 0:1] * rescale + jnp.sum(weights, axis=1, keepdims=True), total.shape
                )
                kept = acc[...] * rescale
            top[...] = jnp.broadcast_to(new, top.shape)
            acc[...] = kept + jnp.dot(
                weights.astype(jnp.bfloat16), vals[behind, head], preferred_element_type=jnp.float32
            )

        fold(0, True)

        def earlier(behind, unused):
            if head == 0:
                key_copy(behind).wait_recv()
            val_copy(behind, head).wait_recv()
            fold(behind, False)
            return unused

        lax.fori_loop(1, me + 1, earlier, 0)
        out_ref[:, here] = (acc[...] / total[...]).astype(jnp.bfloat16)

    for head in range(heads):
        value = columns(lane, head)[...].astype(jnp.float32)
        for away in range(1, tp):
            sum_copy(away, head).wait_recv()
            value = value + parts[away - 1, head].astype(jnp.float32)
        vals[0, head] = value.astype(jnp.bfloat16)

        def hand_on(ahead, unused, head=head):
            val_copy(ahead, head).start()
            return unused

        lax.fori_loop(1, ctx - me, hand_on, 0)
        if head >= 1:
            attend(head - 1)
    attend(heads - 1)

    for head in range(heads):
        for away in range(1, tp):
            sum_copy(away, head).wait_send()

        def sent(ahead, unused, head=head):
            val_copy(ahead, head).wait_send()
            return unused

        lax.fori_loop(1, ctx - me, sent, 0)
    for away in range(1, tp):
        gat_copy(away).wait_send()
    for index in range(2 * chips - 1):
        full_copy(index).wait_send()

    def key_sent(ahead, unused):
        key_copy(ahead).wait_send()
        return unused

    lax.fori_loop(1, ctx - me, key_sent, 0)


def sum_and_attend(gated, share, value_weight, queries, keys):
    ctx, tp = lax.axis_size("ctx"), lax.axis_size("tp")
    rows, width = queries.shape
    heads = width // HD
    return pl.pallas_call(
        functools.partial(attend_kernel, ctx, tp),
        in_specs=[pl.BlockSpec(memory_space=pltpu.VMEM)] * 5,
        out_specs=[pl.BlockSpec(memory_space=pltpu.VMEM)] * 2,
        out_shape=[
            jax.ShapeDtypeStruct((rows, share.shape[2]), jnp.bfloat16),
            jax.ShapeDtypeStruct((rows, width), jnp.bfloat16),
        ],
        scratch_shapes=[
            pltpu.VMEM((tp,) + gated.shape, jnp.bfloat16),
            pltpu.VMEM((tp, ctx) + share.shape[1:], jnp.bfloat16),
            pltpu.VMEM((rows, tp * width), jnp.bfloat16),
            pltpu.VMEM((ctx, rows, width), jnp.bfloat16),
            pltpu.VMEM((tp - 1, heads, rows, HD), jnp.bfloat16),
            pltpu.VMEM((ctx, heads, rows, HD), jnp.bfloat16),
            pltpu.VMEM((rows, HD), jnp.float32),
            pltpu.VMEM((rows, HD), jnp.float32),
            pltpu.VMEM((rows, HD), jnp.float32),
            pltpu.SemaphoreType.DMA((2, tp)),
            pltpu.SemaphoreType.DMA((2, ctx)),
            pltpu.SemaphoreType.DMA((2, ctx)),
            pltpu.SemaphoreType.DMA((2, tp - 1, heads)),
            pltpu.SemaphoreType.DMA((2, ctx, heads)),
        ],
        cost_estimate=pl.CostEstimate(
            flops=4 * rows * ctx * rows * width,
            bytes_accessed=4 * ctx * rows * width,
            transcendentals=0,
        ),
        compiler_params=pltpu.CompilerParams(
            vmem_limit_bytes=48 * 1024 * 1024, collective_id=0, has_side_effects=True
        ),
        name="sum_attend",
    )(gated, share, value_weight, queries, keys)


def shards(
    streams,
    short_filter,
    decay_rates,
    residues,
    skip_gain,
    hyena_weight,
    value_weight,
    queries,
    key_vectors,
):
    ctx, tp = lax.axis_size("ctx"), lax.axis_size("tp")
    rows = streams.shape[1]
    chans, width = hyena_weight.shape
    part = chans // ctx
    share = lax.dynamic_slice(hyena_weight, (lax.axis_index("ctx") * part, 0), (part, width))
    share = share.reshape(part, tp, width // tp).transpose(1, 0, 2)
    share = lax.all_to_all(share, "tp", split_axis=0, concat_axis=0, tiled=True)
    gated = hyena_gated(streams, short_filter, decay_rates.T, residues.T, skip_gain)
    hyena_out, context = sum_and_attend(gated, share, value_weight, queries, key_vectors)
    return (hyena_out, context)


def solution(mesh):
    return jax.shard_map(
        shards,
        mesh=mesh,
        in_specs=(
            P(None, "ctx", "tp"),
            P(None, None, "tp"),
            P("tp", None),
            P("tp", None),
            P("tp"),
            P("tp", None),
            P("tp", None),
            P("ctx", "tp"),
            P("ctx", "tp"),
        ),
        out_specs=(P("ctx", "tp"), P("ctx", "tp")),
        check_vma=False,
    )
```

```python
import functools
import math

import jax
import jax.numpy as jnp
from jax import lax
from jax.experimental import pallas as pl
from jax.experimental.pallas import tpu as pltpu
from jax.sharding import PartitionSpec as P

HD = 128
LANES = 128
SEGS = 8
HALO = 16


def from_behind(value, axis, steps):
    count = lax.axis_size(axis)
    initial, last = (max(0, -steps), min(count, count - steps))
    return lax.ppermute(value, axis, [(source, source + steps) for source in range(initial, last)])


def filter_kernel(prev_ref, streams_ref, taps_ref, rates_ref, gate_ref, u_ref, seg_ref, end_ref, ext):
    rows = streams_ref.shape[1]
    steps = rows // SEGS
    modes = rates_ref.shape[0]
    outs = []
    for s in range(3):
        ext[s, :HALO, :] = prev_ref[s].astype(jnp.float32)
        ext[s, HALO:, :] = streams_ref[s].astype(jnp.float32)
    for s in range(3):
        acc = taps_ref[s, 0:1, :] * ext[s, HALO:, :]
        for j in range(1, 7):
            acc = acc + taps_ref[s, j : j + 1, :] * ext[s, HALO - j : HALO - j + rows, :]
        outs.append(acc)
    gate_ref[...] = outs[0]
    u_ref[...] = outs[1] * outs[2]
    rates = rates_ref[...]
    decay = jnp.exp(-rates)
    factor = [jnp.broadcast_to(decay[n : n + 1], (SEGS, LANES)) for n in range(modes)]
    state = [jnp.zeros((SEGS, LANES), jnp.float32) for _ in range(modes)]
    for step in range(steps):
        here = u_ref[pl.ds(step, SEGS, stride=steps), :]
        for n in range(modes):
            state[n] = state[n] * factor[n] + here
    left = (steps * (SEGS - 1 - lax.broadcasted_iota(jnp.int32, (SEGS, LANES), 0))).astype(jnp.float32)
    for n in range(modes):
        seg_ref[n * SEGS : (n + 1) * SEGS, :] = state[n]
        reach = jnp.exp(-jnp.broadcast_to(rates[n : n + 1], (SEGS, LANES)) * left)
        end_ref[n : n + 1, :] = jnp.sum(reach * state[n], axis=0, keepdims=True)


def mix_kernel(gate_ref, u_ref, seg_ref, inc_ref, rates_ref, res_ref, skip_ref, out_ref, first, mixed):
    rows = u_ref.shape[0]
    steps = rows // SEGS
    modes = rates_ref.shape[0]
    rates = rates_ref[...]
    decay = jnp.exp(-rates)
    hop = jnp.exp(-rates * steps)
    carried = inc_ref[...]
    for seg in range(SEGS):
        first[pl.ds(seg, modes, stride=SEGS), :] = carried
        carried = carried * hop + seg_ref[pl.ds(seg, modes, stride=SEGS), :]
    residue = res_ref[...]
    skip = jnp.broadcast_to(skip_ref[...], (SEGS, LANES))
    factor = [jnp.broadcast_to(decay[n : n + 1], (SEGS, LANES)) for n in range(modes)]
    weight = [jnp.broadcast_to(residue[n : n + 1], (SEGS, LANES)) for n in range(modes)]
    state = [first[n * SEGS : (n + 1) * SEGS, :] for n in range(modes)]
    for step in range(steps):
        where = pl.ds(step, SEGS, stride=steps)
        here = u_ref[where, :]
        terms = [skip * here, None]
        for n in range(modes):
            state[n] = state[n] * factor[n] + here
            term = weight[n] * state[n]
            terms[n % 2] = term if terms[n % 2] is None else terms[n % 2] + term
        mixed[where, :] = gate_ref[where, :] * (terms[0] + terms[1])
    out_ref[...] = mixed[...].astype(jnp.bfloat16)


def hyena_gated(streams, short_filter, rates, residues, skip_gain):
    rows, chans = streams.shape[1:]
    modes = rates.shape[0]
    blocks = chans // LANES
    previous = from_behind(streams[:, rows - HALO :, :], "ctx", 1)
    f32 = jnp.float32
    tok = pl.BlockSpec((rows, LANES), lambda i: (0, i))
    pole = pl.BlockSpec((modes, LANES), lambda i: (0, i))
    seg = pl.BlockSpec((modes * SEGS, LANES), lambda i: (0, i))
    gate, u, seg_state, end_state = pl.pallas_call(
        filter_kernel,
        grid=(blocks,),
        in_specs=[
            pl.BlockSpec((3, HALO, LANES), lambda i: (0, 0, i)),
            pl.BlockSpec((3, rows, LANES), lambda i: (0, 0, i)),
            pl.BlockSpec((3, 7, LANES), lambda i: (0, 0, i)),
            pole,
        ],
        out_specs=[tok, tok, seg, pole],
        out_shape=[
            jax.ShapeDtypeStruct((rows, chans), f32),
            jax.ShapeDtypeStruct((rows, chans), f32),
            jax.ShapeDtypeStruct((modes * SEGS, chans), f32),
            jax.ShapeDtypeStruct((modes, chans), f32),
        ],
        scratch_shapes=[pltpu.VMEM((3, rows + HALO, LANES), f32)],
        cost_estimate=pl.CostEstimate(flops=20_000_000, bytes_accessed=2_500_000, transcendentals=0),
        compiler_params=pltpu.CompilerParams(vmem_limit_bytes=24 * 1024 * 1024),
        name="filter_scan",
    )(previous, streams, short_filter, rates)
    count, mine = lax.axis_size("ctx"), lax.axis_index("ctx")
    ends = lax.all_gather(end_state, "ctx")
    gap = mine - 1 - jnp.arange(count)
    reach = jnp.exp(-rates[None] * (rows * jnp.maximum(gap, 0)).astype(f32)[:, None, None])
    incoming = jnp.sum(jnp.where((gap >= 0)[:, None, None], reach * ends, 0.0), axis=0)
    return pl.pallas_call(
        mix_kernel,
        grid=(blocks,),
        in_specs=[tok, tok, seg, pole, pole, pole, pl.BlockSpec((1, LANES), lambda i: (0, i))],
        out_specs=tok,
        out_shape=jax.ShapeDtypeStruct((rows, chans), jnp.bfloat16),
        scratch_shapes=[pltpu.VMEM((modes * SEGS, LANES), f32), pltpu.VMEM((rows, LANES), f32)],
        cost_estimate=pl.CostEstimate(flops=20_000_000, bytes_accessed=2_500_000, transcendentals=0),
        compiler_params=pltpu.CompilerParams(vmem_limit_bytes=24 * 1024 * 1024),
        name="mix_scan",
    )(gate, u, seg_state, incoming, rates, residues, skip_gain[None])


def attend_kernel(
    ctx,
    tp,
    gated_ref,
    share_ref,
    weight_ref,
    q_ref,
    own_ref,
    hyena_ref,
    out_ref,
    gat,
    full,
    terms_ref,
    keys,
    parts,
    vals,
    acc,
    top,
    total,
    gat_sems,
    full_sems,
    key_sems,
    sum_sems,
    val_sems,
):
    rows, width = q_ref.shape
    heads = width // HD
    scale = 1.0 / math.sqrt(HD)
    me, lane = lax.axis_index("ctx"), lax.axis_index("tp")

    barrier = pltpu.get_barrier_semaphore()
    for away in range(1, tp):
        pl.semaphore_signal(
            barrier,
            inc=1,
            device_id={"tp": lax.rem(lane + away, tp)},
            device_id_type=pl.DeviceIdType.MESH,
        )
    for away in range(1, ctx):
        pl.semaphore_signal(
            barrier,
            inc=1,
            device_id={"ctx": lax.rem(me + away, ctx)},
            device_id_type=pl.DeviceIdType.MESH,
        )
    pl.semaphore_wait(barrier, tp - 1 + ctx - 1)

    def gat_copy(away):
        return pltpu.make_async_remote_copy(
            src_ref=gated_ref,
            dst_ref=gat.at[lane],
            send_sem=gat_sems.at[0, away],
            recv_sem=gat_sems.at[1, away],
            device_id={"tp": lax.rem(lane + away, tp)},
            device_id_type=pl.DeviceIdType.MESH,
        )

    chips = ctx // 2
    chip, core = lax.div(me, 2), lax.rem(me, 2)
    sibling = 2 * chip + 1 - core

    def full_copy(index):
        if index == 0:
            source, block, target = share_ref, me, sibling
        elif index < chips:
            source, block = share_ref, me
            target = 2 * lax.rem(chip + index, chips) + core
        else:
            away = index - chips + 1
            block = 2 * lax.rem(chip + chips - away, chips) + core
            source, target = full.at[:, block], sibling
        return pltpu.make_async_remote_copy(
            src_ref=source,
            dst_ref=full.at[:, block],
            send_sem=full_sems.at[0, index],
            recv_sem=full_sems.at[1, index],
            device_id={"ctx": target},
            device_id_type=pl.DeviceIdType.MESH,
        )

    def later(buffer, sems, source, slot, index, target):
        return pltpu.make_async_remote_copy(
            src_ref=buffer(source),
            dst_ref=buffer(slot),
            send_sem=sems(0, index),
            recv_sem=sems(1, slot),
            device_id={"ctx": target},
            device_id_type=pl.DeviceIdType.MESH,
        )

    def ahead(at, d):
        return later(*at, 0, 2 * d, 2 * d, lax.rem(me + 2 * d, ctx))

    def beside(at):
        return later(*at, 0, 1, 0, sibling)

    def onward(at, d):
        return later(*at, 2 * d, 2 * d + 1 - 2 * core, 2 * d - 1, sibling)

    def loop(first, last, act):
        def body(i, unused):
            act(i)
            return unused

        lax.fori_loop(first, last, body, 0)

    def give(at):
        loop(1, chips - chip, lambda d: ahead(at, d).start())
        loop(0, 1 - core, lambda d: beside(at).start())

    def relay(at):
        def step(d):
            ahead(at, d).wait_recv()
            onward(at, d).start()

        loop(1, chip + 1, step)

    def odd(at, i):
        return later(*at, 0, 2 * i + 1, 0, sibling)

    def take(at):
        loop(0, chip + core, lambda i: odd(at, i).wait_recv())

    def given(at):
        loop(1, chips - chip, lambda d: ahead(at, d).wait_send())
        loop(0, 1 - core, lambda d: beside(at).wait_send())
        loop(1, chip + 1, lambda d: onward(at, d).wait_send())

    key_at = (lambda slot: keys.at[slot], lambda way, i: key_sems.at[way, i])

    def val_at(head):
        return (lambda slot: vals.at[slot, head], lambda way, i: val_sems.at[way, i, head])

    for away in range(1, tp):
        gat_copy(away).start()
    for index in range(1, chips):
        full_copy(index).start()
    full_copy(0).start()

    gat[lane] = gated_ref[...]
    full[:, me] = share_ref[...]
    keys[0] = own_ref[...]
    for index in range(1, chips):
        full_copy(index).wait_recv()
        full_copy(index + chips - 1).start()
    give(key_at)
    for away in range(1, tp):
        gat_copy(away).wait_recv()
    full_copy(0).wait_recv()
    for index in range(chips, 2 * chips - 1):
        full_copy(index).wait_recv()
    chans, wide = gat.shape[2], full.shape[3]
    tile = min(wide, 256)
    for at in range(0, wide, tile):
        summed = None
        for p in range(tp):
            term = jnp.dot(
                gat[p],
                full[p, :, :, at : at + tile].reshape(chans, tile),
                preferred_element_type=jnp.float32,
            )
            summed = term if summed is None else summed + term
        hyena_ref[:, at : at + tile] = summed.astype(jnp.bfloat16)
    for at in range(0, tp * width, width):
        terms_ref[:, at : at + width] = jnp.dot(
            hyena_ref[...], weight_ref[:, at : at + width], preferred_element_type=jnp.float32
        ).astype(jnp.bfloat16)

    def columns(owner, head):
        return terms_ref.at[:, pl.ds(pl.multiple_of(owner * width + head * HD, HD), HD)]

    def sum_copy(away, head):
        owner = lax.rem(lane + away, tp)
        return pltpu.make_async_remote_copy(
            src_ref=columns(owner, head),
            dst_ref=parts.at[away - 1, head],
            send_sem=sum_sems.at[0, away - 1, head],
            recv_sem=sum_sems.at[1, away - 1, head],
            device_id={"tp": owner},
            device_id_type=pl.DeviceIdType.MESH,
        )

    for head in range(heads):
        for away in range(1, tp):
            sum_copy(away, head).start()

    def attend(head):
        here = slice(head * HD, (head + 1) * HD)

        def fold(behind, diagonal):
            scores = (
                lax.dot_general(
                    q_ref[:, here],
                    keys[behind, :, here],
                    (((1,), (1,)), ((), ())),
                    preferred_element_type=jnp.float32,
                )
                * scale
            )
            if diagonal:
                query = lax.broadcasted_iota(jnp.int32, (rows, rows), 0)
                key = lax.broadcasted_iota(jnp.int32, (rows, rows), 1)
                scores = jnp.where(key <= query, scores, -1e30)
                new = jnp.max(scores, axis=1, keepdims=True)
                weights = jnp.exp(scores - new)
                total[...] = jnp.broadcast_to(jnp.sum(weights, axis=1, keepdims=True), total.shape)
                kept = 0.0
            else:
                old = top[:, 0:1]
                new = jnp.maximum(old, jnp.max(scores, axis=1, keepdims=True))
                weights = jnp.exp(scores - new)
                rescale = jnp.exp(old - new)
                total[...] = jnp.broadcast_to(
                    total[:, 0:1] * rescale + jnp.sum(weights, axis=1, keepdims=True), total.shape
                )
                kept = acc[...] * rescale
            top[...] = jnp.broadcast_to(new, top.shape)
            acc[...] = kept + jnp.dot(
                weights.astype(jnp.bfloat16), vals[behind, head], preferred_element_type=jnp.float32
            )

        fold(0, True)

        def earlier(behind, unused):
            fold(behind, False)
            return unused

        lax.fori_loop(1, me + 1, earlier, 0)
        out_ref[:, here] = (acc[...] / total[...]).astype(jnp.bfloat16)

    for head in range(heads):
        value = columns(lane, head)[...].astype(jnp.float32)
        for away in range(1, tp):
            sum_copy(away, head).wait_recv()
            value = value + parts[away - 1, head].astype(jnp.float32)
        vals[0, head] = value.astype(jnp.bfloat16)

        give(val_at(head))
        if head == 0:
            relay(key_at)
            take(key_at)
        else:
            relay(val_at(head - 1))
            take(val_at(head - 1))
            attend(head - 1)
    relay(val_at(heads - 1))
    take(val_at(heads - 1))
    attend(heads - 1)

    for head in range(heads):
        for away in range(1, tp):
            sum_copy(away, head).wait_send()

        given(val_at(head))
    for away in range(1, tp):
        gat_copy(away).wait_send()
    for index in range(2 * chips - 1):
        full_copy(index).wait_send()

    given(key_at)


def sum_and_attend(gated, share, value_weight, queries, keys):
    ctx, tp = lax.axis_size("ctx"), lax.axis_size("tp")
    rows, width = queries.shape
    heads = width // HD
    return pl.pallas_call(
        functools.partial(attend_kernel, ctx, tp),
        in_specs=[pl.BlockSpec(memory_space=pltpu.VMEM)] * 5,
        out_specs=[pl.BlockSpec(memory_space=pltpu.VMEM)] * 2,
        out_shape=[
            jax.ShapeDtypeStruct((rows, share.shape[2]), jnp.bfloat16),
            jax.ShapeDtypeStruct((rows, width), jnp.bfloat16),
        ],
        scratch_shapes=[
            pltpu.VMEM((tp,) + gated.shape, jnp.bfloat16),
            pltpu.VMEM((tp, ctx) + share.shape[1:], jnp.bfloat16),
            pltpu.VMEM((rows, tp * width), jnp.bfloat16),
            pltpu.VMEM((ctx, rows, width), jnp.bfloat16),
            pltpu.VMEM((tp - 1, heads, rows, HD), jnp.bfloat16),
            pltpu.VMEM((ctx, heads, rows, HD), jnp.bfloat16),
            pltpu.VMEM((rows, HD), jnp.float32),
            pltpu.VMEM((rows, HD), jnp.float32),
            pltpu.VMEM((rows, HD), jnp.float32),
            pltpu.SemaphoreType.DMA((2, tp)),
            pltpu.SemaphoreType.DMA((2, ctx)),
            pltpu.SemaphoreType.DMA((2, ctx)),
            pltpu.SemaphoreType.DMA((2, tp - 1, heads)),
            pltpu.SemaphoreType.DMA((2, ctx, heads)),
        ],
        cost_estimate=pl.CostEstimate(
            flops=4 * rows * ctx * rows * width,
            bytes_accessed=4 * ctx * rows * width,
            transcendentals=0,
        ),
        compiler_params=pltpu.CompilerParams(
            vmem_limit_bytes=48 * 1024 * 1024, collective_id=0, has_side_effects=True
        ),
        name="sum_attend",
    )(gated, share, value_weight, queries, keys)


def shards(
    streams,
    short_filter,
    decay_rates,
    residues,
    skip_gain,
    hyena_weight,
    value_weight,
    queries,
    key_vectors,
):
    ctx, tp = lax.axis_size("ctx"), lax.axis_size("tp")
    rows = streams.shape[1]
    chans, width = hyena_weight.shape
    part = chans // ctx
    share = lax.dynamic_slice(hyena_weight, (lax.axis_index("ctx") * part, 0), (part, width))
    share = share.reshape(part, tp, width // tp).transpose(1, 0, 2)
    share = lax.all_to_all(share, "tp", split_axis=0, concat_axis=0, tiled=True)
    gated = hyena_gated(streams, short_filter, decay_rates.T, residues.T, skip_gain)
    hyena_out, context = sum_and_attend(gated, share, value_weight, queries, key_vectors)
    return (hyena_out, context)


def solution(mesh):
    return jax.shard_map(
        shards,
        mesh=mesh,
        in_specs=(
            P(None, "ctx", "tp"),
            P(None, None, "tp"),
            P("tp", None),
            P("tp", None),
            P("tp"),
            P("tp", None),
            P("tp", None),
            P("ctx", "tp"),
            P("ctx", "tp"),
        ),
        out_specs=(P("ctx", "tp"), P("ctx", "tp")),
        check_vma=False,
    )
```

```python
import functools
import math

import jax
import jax.numpy as jnp
from jax import lax
from jax.experimental import pallas as pl
from jax.experimental.pallas import tpu as pltpu
from jax.sharding import PartitionSpec as P

HD = 128
LANES = 128
SEGS = 8
HALO = 16


def from_behind(value, axis, steps):
    count = lax.axis_size(axis)
    initial, last = (max(0, -steps), min(count, count - steps))
    return lax.ppermute(value, axis, [(source, source + steps) for source in range(initial, last)])


def filter_kernel(prev_ref, streams_ref, taps_ref, rates_ref, gate_ref, u_ref, seg_ref, end_ref, ext):
    rows = streams_ref.shape[1]
    steps = rows // SEGS
    modes = rates_ref.shape[0]
    outs = []
    for s in range(3):
        ext[s, :HALO, :] = prev_ref[s].astype(jnp.float32)
        ext[s, HALO:, :] = streams_ref[s].astype(jnp.float32)
    for s in range(3):
        acc = taps_ref[s, 0:1, :] * ext[s, HALO:, :]
        for j in range(1, 7):
            acc = acc + taps_ref[s, j : j + 1, :] * ext[s, HALO - j : HALO - j + rows, :]
        outs.append(acc)
    gate_ref[...] = outs[0]
    u_ref[...] = outs[1] * outs[2]
    rates = rates_ref[...]
    decay = jnp.exp(-rates)
    factor = [jnp.broadcast_to(decay[n : n + 1], (SEGS, LANES)) for n in range(modes)]
    state = [jnp.zeros((SEGS, LANES), jnp.float32) for _ in range(modes)]
    for step in range(steps):
        here = u_ref[pl.ds(step, SEGS, stride=steps), :]
        for n in range(modes):
            state[n] = state[n] * factor[n] + here
    left = (steps * (SEGS - 1 - lax.broadcasted_iota(jnp.int32, (SEGS, LANES), 0))).astype(jnp.float32)
    for n in range(modes):
        seg_ref[n * SEGS : (n + 1) * SEGS, :] = state[n]
        reach = jnp.exp(-jnp.broadcast_to(rates[n : n + 1], (SEGS, LANES)) * left)
        end_ref[n : n + 1, :] = jnp.sum(reach * state[n], axis=0, keepdims=True)


def mix_kernel(gate_ref, u_ref, seg_ref, inc_ref, rates_ref, res_ref, skip_ref, out_ref, first, mixed):
    rows = u_ref.shape[0]
    steps = rows // SEGS
    modes = rates_ref.shape[0]
    rates = rates_ref[...]
    decay = jnp.exp(-rates)
    hop = jnp.exp(-rates * steps)
    carried = inc_ref[...]
    for seg in range(SEGS):
        first[pl.ds(seg, modes, stride=SEGS), :] = carried
        carried = carried * hop + seg_ref[pl.ds(seg, modes, stride=SEGS), :]
    residue = res_ref[...]
    skip = jnp.broadcast_to(skip_ref[...], (SEGS, LANES))
    factor = [jnp.broadcast_to(decay[n : n + 1], (SEGS, LANES)) for n in range(modes)]
    weight = [jnp.broadcast_to(residue[n : n + 1], (SEGS, LANES)) for n in range(modes)]
    state = [first[n * SEGS : (n + 1) * SEGS, :] for n in range(modes)]
    for step in range(steps):
        where = pl.ds(step, SEGS, stride=steps)
        here = u_ref[where, :]
        terms = [skip * here, None]
        for n in range(modes):
            state[n] = state[n] * factor[n] + here
            term = weight[n] * state[n]
            terms[n % 2] = term if terms[n % 2] is None else terms[n % 2] + term
        mixed[where, :] = gate_ref[where, :] * (terms[0] + terms[1])
    out_ref[...] = mixed[...].astype(jnp.bfloat16)


def hyena_gated(streams, short_filter, rates, residues, skip_gain):
    rows, chans = streams.shape[1:]
    modes = rates.shape[0]
    blocks = chans // LANES
    previous = from_behind(streams[:, rows - HALO :, :], "ctx", 1)
    f32 = jnp.float32
    tok = pl.BlockSpec((rows, LANES), lambda i: (0, i))
    pole = pl.BlockSpec((modes, LANES), lambda i: (0, i))
    seg = pl.BlockSpec((modes * SEGS, LANES), lambda i: (0, i))
    gate, u, seg_state, end_state = pl.pallas_call(
        filter_kernel,
        grid=(blocks,),
        in_specs=[
            pl.BlockSpec((3, HALO, LANES), lambda i: (0, 0, i)),
            pl.BlockSpec((3, rows, LANES), lambda i: (0, 0, i)),
            pl.BlockSpec((3, 7, LANES), lambda i: (0, 0, i)),
            pole,
        ],
        out_specs=[tok, tok, seg, pole],
        out_shape=[
            jax.ShapeDtypeStruct((rows, chans), f32),
            jax.ShapeDtypeStruct((rows, chans), f32),
            jax.ShapeDtypeStruct((modes * SEGS, chans), f32),
            jax.ShapeDtypeStruct((modes, chans), f32),
        ],
        scratch_shapes=[pltpu.VMEM((3, rows + HALO, LANES), f32)],
        cost_estimate=pl.CostEstimate(flops=20_000_000, bytes_accessed=2_500_000, transcendentals=0),
        compiler_params=pltpu.CompilerParams(vmem_limit_bytes=24 * 1024 * 1024),
        name="filter_scan",
    )(previous, streams, short_filter, rates)
    count, mine = lax.axis_size("ctx"), lax.axis_index("ctx")
    ends = lax.all_gather(end_state, "ctx")
    gap = mine - 1 - jnp.arange(count)
    reach = jnp.exp(-rates[None] * (rows * jnp.maximum(gap, 0)).astype(f32)[:, None, None])
    incoming = jnp.sum(jnp.where((gap >= 0)[:, None, None], reach * ends, 0.0), axis=0)
    return pl.pallas_call(
        mix_kernel,
        grid=(blocks,),
        in_specs=[tok, tok, seg, pole, pole, pole, pl.BlockSpec((1, LANES), lambda i: (0, i))],
        out_specs=tok,
        out_shape=jax.ShapeDtypeStruct((rows, chans), jnp.bfloat16),
        scratch_shapes=[pltpu.VMEM((modes * SEGS, LANES), f32), pltpu.VMEM((rows, LANES), f32)],
        cost_estimate=pl.CostEstimate(flops=20_000_000, bytes_accessed=2_500_000, transcendentals=0),
        compiler_params=pltpu.CompilerParams(vmem_limit_bytes=24 * 1024 * 1024),
        name="mix_scan",
    )(gate, u, seg_state, incoming, rates, residues, skip_gain[None])


def attend_kernel(
    ctx,
    tp,
    gated_ref,
    share_ref,
    weight_ref,
    q_ref,
    own_ref,
    hyena_ref,
    out_ref,
    gat,
    full,
    terms_ref,
    keys,
    parts,
    vals,
    acc,
    top,
    total,
    gat_sems,
    full_sems,
    key_sems,
    sum_sems,
    val_sems,
):
    rows, width = q_ref.shape
    heads = width // HD
    scale = 1.0 / math.sqrt(HD)
    me, lane = lax.axis_index("ctx"), lax.axis_index("tp")

    barrier = pltpu.get_barrier_semaphore()
    for away in range(1, tp):
        pl.semaphore_signal(
            barrier,
            inc=1,
            device_id={"tp": lax.rem(lane + away, tp)},
            device_id_type=pl.DeviceIdType.MESH,
        )
    for away in range(1, ctx):
        pl.semaphore_signal(
            barrier,
            inc=1,
            device_id={"ctx": lax.rem(me + away, ctx)},
            device_id_type=pl.DeviceIdType.MESH,
        )
    pl.semaphore_wait(barrier, tp - 1 + ctx - 1)

    def gat_copy(away):
        return pltpu.make_async_remote_copy(
            src_ref=gated_ref,
            dst_ref=gat.at[lane],
            send_sem=gat_sems.at[0, away],
            recv_sem=gat_sems.at[1, away],
            device_id={"tp": lax.rem(lane + away, tp)},
            device_id_type=pl.DeviceIdType.MESH,
        )

    chips = ctx // 2
    chip, core = lax.div(me, 2), lax.rem(me, 2)
    sibling = 2 * chip + 1 - core

    def full_copy(index):
        if index == 0:
            source, block, target = share_ref, me, sibling
        elif index < chips:
            source, block = share_ref, me
            target = 2 * lax.rem(chip + index, chips) + core
        else:
            away = index - chips + 1
            block = 2 * lax.rem(chip + chips - away, chips) + core
            source, target = full.at[:, block], sibling
        return pltpu.make_async_remote_copy(
            src_ref=source,
            dst_ref=full.at[:, block],
            send_sem=full_sems.at[0, index],
            recv_sem=full_sems.at[1, index],
            device_id={"ctx": target},
            device_id_type=pl.DeviceIdType.MESH,
        )

    def later(buffer, sems, source, slot, index, target):
        return pltpu.make_async_remote_copy(
            src_ref=buffer(source),
            dst_ref=buffer(slot),
            send_sem=sems(0, index),
            recv_sem=sems(1, slot),
            device_id={"ctx": target},
            device_id_type=pl.DeviceIdType.MESH,
        )

    def ahead(at, d):
        return later(*at, 0, 2 * d, 2 * d, lax.rem(me + 2 * d, ctx))

    def beside(at):
        return later(*at, 0, 1, 0, sibling)

    def onward(at, d):
        return later(*at, 2 * d, 2 * d + 1 - 2 * core, 2 * d - 1, sibling)

    def loop(first, last, act):
        def body(i, unused):
            act(i)
            return unused

        lax.fori_loop(first, last, body, 0)

    def give(at):
        loop(1, chips - chip, lambda d: ahead(at, d).start())
        loop(0, 1 - core, lambda d: beside(at).start())

    def relay(at):
        def step(d):
            ahead(at, d).wait_recv()
            onward(at, d).start()

        loop(1, chip + 1, step)

    def odd(at, i):
        return later(*at, 0, 2 * i + 1, 0, sibling)

    def take(at):
        loop(0, chip + core, lambda i: odd(at, i).wait_recv())

    def given(at):
        loop(1, chips - chip, lambda d: ahead(at, d).wait_send())
        loop(0, 1 - core, lambda d: beside(at).wait_send())
        loop(1, chip + 1, lambda d: onward(at, d).wait_send())

    key_at = (lambda slot: keys.at[slot], lambda way, i: key_sems.at[way, i])

    def val_at(head):
        return (lambda slot: vals.at[slot, head], lambda way, i: val_sems.at[way, i, head])

    for away in range(1, tp):
        gat_copy(away).start()
    for index in range(1, chips):
        full_copy(index).start()
    full_copy(0).start()

    gat[lane] = gated_ref[...]
    full[:, me] = share_ref[...]
    keys[0] = own_ref[...]
    for index in range(1, chips):
        full_copy(index).wait_recv()
        full_copy(index + chips - 1).start()
    give(key_at)
    for away in range(1, tp):
        gat_copy(away).wait_recv()
    full_copy(0).wait_recv()
    for index in range(chips, 2 * chips - 1):
        full_copy(index).wait_recv()
    chans, wide = gat.shape[2], full.shape[3]
    tile = min(wide, 256)
    for at in range(0, wide, tile):
        summed = None
        for p in range(tp):
            term = jnp.dot(
                gat[p],
                full[p, :, :, at : at + tile].reshape(chans, tile),
                preferred_element_type=jnp.float32,
            )
            summed = term if summed is None else summed + term
        hyena_ref[:, at : at + tile] = summed.astype(jnp.bfloat16)
    for at in range(0, tp * width, width):
        terms_ref[:, at : at + width] = jnp.dot(
            hyena_ref[...], weight_ref[:, at : at + width], preferred_element_type=jnp.float32
        ).astype(jnp.bfloat16)

    def columns(owner, head):
        return terms_ref.at[:, pl.ds(pl.multiple_of(owner * width + head * HD, HD), HD)]

    def sum_copy(away, head):
        owner = lax.rem(lane + away, tp)
        return pltpu.make_async_remote_copy(
            src_ref=columns(owner, head),
            dst_ref=parts.at[away - 1, head],
            send_sem=sum_sems.at[0, away - 1, head],
            recv_sem=sum_sems.at[1, away - 1, head],
            device_id={"tp": owner},
            device_id_type=pl.DeviceIdType.MESH,
        )

    for head in range(heads):
        for away in range(1, tp):
            sum_copy(away, head).start()

    def attend(head):
        here = slice(head * HD, (head + 1) * HD)

        def fold(behind, diagonal):
            scores = (
                lax.dot_general(
                    q_ref[:, here],
                    keys[behind, :, here],
                    (((1,), (1,)), ((), ())),
                    preferred_element_type=jnp.float32,
                )
                * scale
            )
            if diagonal:
                query = lax.broadcasted_iota(jnp.int32, (rows, rows), 0)
                key = lax.broadcasted_iota(jnp.int32, (rows, rows), 1)
                scores = jnp.where(key <= query, scores, -1e30)
                new = jnp.max(scores, axis=1, keepdims=True)
                weights = jnp.exp(scores - new)
                total[...] = jnp.broadcast_to(jnp.sum(weights, axis=1, keepdims=True), total.shape)
                kept = 0.0
            else:
                old = top[:, 0:1]
                new = jnp.maximum(old, jnp.max(scores, axis=1, keepdims=True))
                weights = jnp.exp(scores - new)
                rescale = jnp.exp(old - new)
                total[...] = jnp.broadcast_to(
                    total[:, 0:1] * rescale + jnp.sum(weights, axis=1, keepdims=True), total.shape
                )
                kept = acc[...] * rescale
            top[...] = jnp.broadcast_to(new, top.shape)
            acc[...] = kept + jnp.dot(
                weights.astype(jnp.bfloat16), vals[behind, head], preferred_element_type=jnp.float32
            )

        fold(0, True)

        def earlier(behind, unused):
            fold(behind, False)
            return unused

        lax.fori_loop(1, me + 1, earlier, 0)
        out_ref[:, here] = (acc[...] / total[...]).astype(jnp.bfloat16)

    for head in range(heads):
        value = columns(lane, head)[...].astype(jnp.float32)
        for away in range(1, tp):
            sum_copy(away, head).wait_recv()
            value = value + parts[away - 1, head].astype(jnp.float32)
        vals[0, head] = value.astype(jnp.bfloat16)

        give(val_at(head))
        relay(key_at if head == 0 else val_at(head - 1))
        if head >= 2:
            if head == 2:
                take(key_at)
            take(val_at(head - 2))
            attend(head - 2)
    relay(val_at(heads - 1))
    if heads <= 2:
        take(key_at)
    for head in range(max(heads - 2, 0), heads):
        take(val_at(head))
        attend(head)

    for head in range(heads):
        for away in range(1, tp):
            sum_copy(away, head).wait_send()

        given(val_at(head))
    for away in range(1, tp):
        gat_copy(away).wait_send()
    for index in range(2 * chips - 1):
        full_copy(index).wait_send()

    given(key_at)


def sum_and_attend(gated, share, value_weight, queries, keys):
    ctx, tp = lax.axis_size("ctx"), lax.axis_size("tp")
    rows, width = queries.shape
    heads = width // HD
    return pl.pallas_call(
        functools.partial(attend_kernel, ctx, tp),
        in_specs=[pl.BlockSpec(memory_space=pltpu.VMEM)] * 5,
        out_specs=[pl.BlockSpec(memory_space=pltpu.VMEM)] * 2,
        out_shape=[
            jax.ShapeDtypeStruct((rows, share.shape[2]), jnp.bfloat16),
            jax.ShapeDtypeStruct((rows, width), jnp.bfloat16),
        ],
        scratch_shapes=[
            pltpu.VMEM((tp,) + gated.shape, jnp.bfloat16),
            pltpu.VMEM((tp, ctx) + share.shape[1:], jnp.bfloat16),
            pltpu.VMEM((rows, tp * width), jnp.bfloat16),
            pltpu.VMEM((ctx, rows, width), jnp.bfloat16),
            pltpu.VMEM((tp - 1, heads, rows, HD), jnp.bfloat16),
            pltpu.VMEM((ctx, heads, rows, HD), jnp.bfloat16),
            pltpu.VMEM((rows, HD), jnp.float32),
            pltpu.VMEM((rows, HD), jnp.float32),
            pltpu.VMEM((rows, HD), jnp.float32),
            pltpu.SemaphoreType.DMA((2, tp)),
            pltpu.SemaphoreType.DMA((2, ctx)),
            pltpu.SemaphoreType.DMA((2, ctx)),
            pltpu.SemaphoreType.DMA((2, tp - 1, heads)),
            pltpu.SemaphoreType.DMA((2, ctx, heads)),
        ],
        cost_estimate=pl.CostEstimate(
            flops=4 * rows * ctx * rows * width,
            bytes_accessed=4 * ctx * rows * width,
            transcendentals=0,
        ),
        compiler_params=pltpu.CompilerParams(
            vmem_limit_bytes=48 * 1024 * 1024, collective_id=0, has_side_effects=True
        ),
        name="sum_attend",
    )(gated, share, value_weight, queries, keys)


def shards(
    streams,
    short_filter,
    decay_rates,
    residues,
    skip_gain,
    hyena_weight,
    value_weight,
    queries,
    key_vectors,
):
    ctx, tp = lax.axis_size("ctx"), lax.axis_size("tp")
    rows = streams.shape[1]
    chans, width = hyena_weight.shape
    part = chans // ctx
    share = lax.dynamic_slice(hyena_weight, (lax.axis_index("ctx") * part, 0), (part, width))
    share = share.reshape(part, tp, width // tp).transpose(1, 0, 2)
    share = lax.all_to_all(share, "tp", split_axis=0, concat_axis=0, tiled=True)
    gated = hyena_gated(streams, short_filter, decay_rates.T, residues.T, skip_gain)
    hyena_out, context = sum_and_attend(gated, share, value_weight, queries, key_vectors)
    return (hyena_out, context)


def solution(mesh):
    return jax.shard_map(
        shards,
        mesh=mesh,
        in_specs=(
            P(None, "ctx", "tp"),
            P(None, None, "tp"),
            P("tp", None),
            P("tp", None),
            P("tp"),
            P("tp", None),
            P("tp", None),
            P("ctx", "tp"),
            P("ctx", "tp"),
        ),
        out_specs=(P("ctx", "tp"), P("ctx", "tp")),
        check_vma=False,
    )
```
